128 devices in a mesh: row: 8 (over z, core), col: 16 (over x, y).
Axes of the slice: x: 4, y: 4, z: 4, core: 2. Of those that a mesh axis runs over, the one named last changes fastest.
Arguments:
- normed: bfloat16 [1024, 8192], P('col', 'row'), may hold values from -16 to 16, as said below
- w_qkv: bfloat16 [3, 8192, 8192], P(None, 'row', 'col'), as said below
- w_out: bfloat16 [8192, 8192], P('col', 'row'), may hold values from -0.0625 to 0.0625
- doc_start: int32 [8], replicated, may hold values from 0 to 896, as said below
- grad_y: bfloat16 [1024, 8192], P('col', 'row'), may hold values from -6 to 6
Outputs:
- layer_out: bfloat16 [1024, 8192], P('col', 'row')
- grad_x: bfloat16 [1024, 8192], P('col', 'row')
- grad_qkv: float32 [3, 8192, 8192], P(None, 'row', 'col')
- grad_out: float32 [8192, 8192], P('col', 'row')
The draws below stay inside these ranges and needn't reach their ends.
Inputs may be any that keep to these rules, and one draw needn't show every extreme that they name: doc_start[b] is a multiple of 128, at most b * 128, never falling, and equal either to b * 128 (block b opens a document) or to doc_start[b - 1]; doc_start[0] = 0 and the last block opens a document. `normed`: activations of order one. `w_qkv`: entries of standard deviation about 1 / sqrt(8192).
All inputs are finite; a program needn't handle non-finite values.
Results may differ from the reference program's by a relative error of at most 0.034.
Values may be sent and summed in bfloat16 or wider, within the bound.
No kernel may reach another device: no remote copies, remote signals or barrier semaphores. Data moves between devices by JAX's collectives and lax.ppermute only.
A program may use at most 128 MiB of HBM per device.

```python
import math
import jax
import jax.numpy as jnp
from jax import lax

D = 8192
HEADS = 64
HD = 128
BLOCK = 128
TOKENS = 1024
ATT = 8192
GROUP_W = 512
N_COL = 16


def draw_doc_start(key, part):
    key = jax.random.fold_in(key, 11)
    block_count = TOKENS // BLOCK
    block_ids = jnp.arange(block_count, dtype=jnp.int32)
    opens = jax.random.randint(key, (block_count,), 0, 6) == 0
    opens = opens | (block_ids == 0) | (block_ids == block_count - 1)
    starts = jnp.where(opens, block_ids * BLOCK, 0)
    return lax.cummax(starts, axis=0).astype(jnp.int32)


def draw_normed(key, part):
    key = jax.random.fold_in(key, 21)
    key_one = jax.random.fold_in(key, 0)
    return jnp.clip(jax.random.normal(key_one, (TOKENS, D), jnp.float32), -6.0, 6.0).astype(jnp.bfloat16)


def draw_w_qkv(key, part):
    key = jax.random.fold_in(key, 31)
    key_one, key_two, key_three = jax.random.split(key, 3)
    shape = (D, ATT)
    spread = 1.0 / math.sqrt(D)
    w_query = jnp.clip(jax.random.normal(key_one, shape, jnp.float32), -6.0, 6.0) * spread
    w_key = jnp.clip(jax.random.normal(key_two, shape, jnp.float32), -6.0, 6.0) * spread
    w_value = jnp.clip(jax.random.normal(key_three, shape, jnp.float32), -6.0, 6.0) * spread
    return jnp.stack([w_query, w_key, w_value]).astype(jnp.bfloat16)


def levels(rng, dims, shards, least, largest):
    level, own = 1.0, jax.random.fold_in(rng, 6)
    for dim, shards_of in shards:
        steps = jnp.exp(jax.random.uniform(jax.random.fold_in(own, dim), (shards_of,), jnp.float32, least / len(shards), largest / len(shards)))
        level = level * jnp.repeat(steps, dims[dim] // shards_of).reshape([-1 if axis == dim else 1 for axis in range(len(dims))])
    return level


def centred(key, extent, scale, limit, cuts=(), held_as=jnp.bfloat16):
    gain = levels(key, extent, cuts, -0.22, 0.18) if cuts else 1.0
    result = jax.random.normal(key, extent, jnp.float32) * scale * gain
    return jnp.minimum(jnp.maximum(result, -limit), limit).astype(held_as)


def setup_inputs(seed: int = 0) -> dict:
    key_of = jax.random.split(jax.random.key(seed), 6)
    normed = draw_normed(jax.random.fold_in(key_of[5], 71), 0)
    w_qkv = draw_w_qkv(jax.random.fold_in(key_of[5], 71), 0)
    w_out = centred(key_of[2], (ATT, D), ATT ** -0.5, 0.0625, ((0, 16), (1, 8)))
    doc_start = draw_doc_start(jax.random.fold_in(key_of[5], 71), 0)
    grad_y = centred(key_of[4], (TOKENS, D), 1.0, 6.0, ((0, 16), (1, 8)))
    return {"normed": normed, "w_qkv": w_qkv, "w_out": w_out, "doc_start": doc_start, "grad_y": grad_y}


neg_big = -1e+30
precise = lax.Precision.HIGHEST

def head_major(matrix):
    return matrix.reshape(TOKENS, HEADS, HD).transpose(1, 0, 2)

def token_major(stacked):
    return stacked.transpose(1, 0, 2).reshape(TOKENS, ATT)

def reference(normed, w_qkv, w_out, doc_start, grad_y):
    score_scale = 1.0 / math.sqrt(HD)
    projected = [jnp.dot(normed, w_qkv[which], preferred_element_type=jnp.float32).astype(jnp.bfloat16) for which in range(3)]
    query_all = head_major(projected[0])
    key_all = head_major(projected[1])
    value_all = head_major(projected[2])
    positions = jnp.arange(TOKENS, dtype=jnp.int32)
    doc_first = jnp.repeat(doc_start, BLOCK)
    allowed = (positions[None, :] >= doc_first[:, None]) & (positions[None, :] <= positions[:, None])

    def forward_head(inputs):
        queries, key_rows, value_rows = inputs
        scores = jnp.dot(queries, key_rows.T, preferred_element_type=jnp.float32) * score_scale
        scores = jnp.where(allowed, scores, neg_big)
        row_max = lax.optimization_barrier(jnp.max(scores, axis=1))
        weights = jnp.where(allowed, jnp.exp(scores - row_max[:, None]), 0.0)
        weight_sum = lax.optimization_barrier(jnp.sum(weights, axis=1))
        blended = jnp.dot(weights.astype(jnp.bfloat16), value_rows, preferred_element_type=jnp.float32) / weight_sum[:, None]
        return (blended, row_max + jnp.log(weight_sum))
    blended_heads, log_total = lax.map(forward_head, (query_all, key_all, value_all))
    attention = token_major(blended_heads).astype(jnp.bfloat16)
    attention_groups = attention.reshape(TOKENS, N_COL, GROUP_W)
    out_groups = w_out.reshape(N_COL, GROUP_W, D)

    def add_group(running, group):
        partial_sum = jnp.dot(attention_groups[:, group], out_groups[group], preferred_element_type=jnp.float32).astype(jnp.bfloat16)
        return (running + lax.optimization_barrier(partial_sum).astype(jnp.float32), None)
    summed = lax.scan(add_group, jnp.zeros((TOKENS, D), jnp.float32), jnp.arange(N_COL, dtype=jnp.int32))[0]
    layer_out = summed.astype(jnp.bfloat16)
    grad_attention = jnp.dot(grad_y, w_out.T, preferred_element_type=jnp.float32).astype(jnp.bfloat16)
    grad_out = jnp.dot(attention.T, grad_y, preferred_element_type=jnp.float32)

    def backward_head(inputs):
        queries, key_rows, value_rows, grad_rows, out_rows, log_rows = inputs
        scores = jnp.dot(queries, key_rows.T, preferred_element_type=jnp.float32) * score_scale
        scores = jnp.where(allowed, scores, neg_big)
        probs = jnp.where(allowed, jnp.exp(scores - log_rows[:, None]), 0.0)
        grad_probs = jnp.dot(grad_rows, value_rows.T, preferred_element_type=jnp.float32)
        row_delta = lax.optimization_barrier(jnp.sum(grad_rows.astype(jnp.float32) * out_rows.astype(jnp.float32), axis=1))
        grad_scores = (probs * (grad_probs - row_delta[:, None])).astype(jnp.bfloat16)
        probs_low = probs.astype(jnp.bfloat16)
        grad_query = jnp.dot(grad_scores, key_rows, preferred_element_type=jnp.float32) * score_scale
        grad_key = jnp.dot(grad_scores.T, queries, preferred_element_type=jnp.float32) * score_scale
        grad_value = jnp.dot(probs_low.T, grad_rows, preferred_element_type=jnp.float32)
        return (grad_query, grad_key, grad_value)
    gradients = lax.map(backward_head, (query_all, key_all, value_all, head_major(grad_attention), head_major(attention), log_total))
    grad_proj = jnp.stack([token_major(matrix_part).astype(jnp.bfloat16) for matrix_part in gradients])
    grad_qkv = jnp.stack([jnp.dot(normed.T, grad_proj[which], preferred_element_type=jnp.float32) for which in range(3)])
    grad_groups = grad_proj.reshape(3, TOKENS, N_COL, GROUP_W)
    weight_groups = w_qkv.reshape(3, D, N_COL, GROUP_W)

    def add_input(running, group):
        partial_sum = jnp.einsum('ctn,ckn->tk', grad_groups[:, :, group].astype(jnp.float32), weight_groups[:, :, group].astype(jnp.float32), precision=precise).astype(jnp.bfloat16)
        return (running + lax.optimization_barrier(partial_sum).astype(jnp.float32), None)
    grad_sum = lax.scan(add_input, jnp.zeros((TOKENS, D), jnp.float32), jnp.arange(N_COL, dtype=jnp.int32))[0]
    grad_x = grad_sum.astype(jnp.bfloat16)
    return (layer_out, grad_x, grad_qkv, grad_out)
```

```python
import math

import jax
import jax.numpy as jnp
from jax import lax
from jax.sharding import PartitionSpec as P

HD = 128
BLOCK = 128
NEG = -1e30
F32 = jnp.float32
BF16 = jnp.bfloat16

RING = 4
CORES = 2


def to_x(value, step):
    pairs = [(c, (c // RING + step) % RING * RING + c % RING) for c in range(RING * RING)]
    return lax.ppermute(value, "col", pairs)


def to_y(value, step):
    pairs = [(c, c // RING * RING + (c % RING + step) % RING) for c in range(RING * RING)]
    return lax.ppermute(value, "col", pairs)


def to_z(value, step):
    pairs = [(r, (r // CORES + step) % RING * CORES + r % CORES) for r in range(RING * CORES)]
    return lax.ppermute(value, "row", pairs)


def swap_cores(value):
    pairs = [(r, r // CORES * CORES + 1 - r % CORES) for r in range(RING * CORES)]
    return lax.ppermute(value, "row", pairs)


def halves_by_core(core, rows):
    half = rows.shape[0] // 2
    return jnp.where(core == 0, rows, jnp.concatenate([rows[half:], rows[:half]], axis=0))


def gather_col(block, core):
    along_x = [block] + [to_x(block, -step) for step in range(1, RING)]
    own = halves_by_core(core, jnp.concatenate(along_x, axis=0))
    along_y = [own] + [to_y(own, -step) for step in range(1, RING)]
    half = own.shape[0] // 2
    mine = jnp.concatenate([part[:half] for part in along_y], axis=0)
    other = jnp.concatenate([part[half:] for part in along_y], axis=0)
    return mine, other


def scatter_sum_row(mine, other, weights):
    received = swap_cores(jnp.dot(other, weights, preferred_element_type=F32).astype(BF16))
    own = jnp.dot(mine, weights, preferred_element_type=F32) + received.astype(F32)
    low = own.astype(BF16)
    width = weights.shape[1] // RING
    total = own[:, :width]
    for step in range(1, RING):
        total = total + to_z(low[:, step * width : (step + 1) * width], step).astype(F32)
    return total.astype(BF16)


def gather_row(block):
    mine = jnp.concatenate([block] + [to_z(block, -step) for step in range(1, RING)], axis=1)
    return mine, swap_cores(mine)


def scatter_sum_col(mine, other, weights, core):
    rows = mine.shape[0] // RING

    def piece(step):
        both = jnp.concatenate(
            [mine[step * rows : (step + 1) * rows], other[step * rows : (step + 1) * rows]], axis=0
        )
        return lax.dot_general(
            both, weights, (((1,), (1,)), ((), ())), preferred_element_type=F32
        )

    arrived = [to_y(piece(step).astype(BF16), step) for step in (2, 1, 3)]
    total = piece(0)
    for part in arrived:
        total = total + part.astype(F32)
    total = halves_by_core(core, total)
    low = total.astype(BF16)
    rows = low.shape[0] // RING
    result = total[:rows]
    for step in range(1, RING):
        result = result + to_x(low[step * rows : (step + 1) * rows], step).astype(F32)
    return result.astype(BF16)


def turned(pieces, shift):
    stacked = jnp.stack(pieces + pieces)
    return lax.dynamic_slice_in_dim(stacked, shift, len(pieces), axis=0)


def on_device(normed, w_qkv, w_out, doc_start, grad_y):
    row_id, col_id = lax.axis_index("row"), lax.axis_index("col")
    z_id, core = row_id // CORES, row_id % CORES
    x_id, y_id = col_id // RING, col_id % RING
    scale = 1.0 / math.sqrt(HD)
    tok_col = normed.shape[0]
    features = normed.shape[1]

    def head_of(step):
        return (z_id + step) % RING * HD

    w_rel = jnp.concatenate(
        [
            lax.dynamic_slice_in_dim(w_qkv[which], head_of(step), HD, axis=1)
            for step in range(RING)
            for which in range(3)
        ],
        axis=1,
    )
    w_out_rel = jnp.concatenate(
        [lax.dynamic_slice_in_dim(w_out, head_of(step), HD, axis=0) for step in range(RING)], axis=0
    )

    x_mine, x_other = gather_col(normed, core)
    qkv = scatter_sum_row(x_mine, x_other, w_rel)
    dy_mine, dy_other = gather_col(grad_y, core)
    grad_rows = scatter_sum_row(dy_mine, dy_other, w_out_rel.T)

    queries = qkv[:, :HD]
    kv_mine = qkv[:, HD:]
    kv = jnp.concatenate([kv_mine, swap_cores(kv_mine)], axis=0)
    keys, values = kv[:, :HD], kv[:, HD:]

    def positions(first_dx):
        dy = jnp.arange(RING, dtype=jnp.int32)[:, None, None]
        dx = first_dx + jnp.arange(RING // 2, dtype=jnp.int32)[None, :, None]
        token = jnp.arange(tok_col, dtype=jnp.int32)[None, None, :]
        device = (x_id + dx) % RING * RING + (y_id + dy) % RING
        return (device * tok_col + token).reshape(-1)

    query_pos = positions(core * 2)
    key_pos = jnp.concatenate([query_pos, positions(core * 2 + 2)])
    block_ids = jnp.arange(doc_start.shape[0], dtype=jnp.int32)
    matched = query_pos[:, None] // BLOCK == block_ids[None, :]
    first_pos = jnp.sum(jnp.where(matched, doc_start[None, :], 0), axis=1)
    allowed = (key_pos[None, :] >= first_pos[:, None]) & (key_pos[None, :] <= query_pos[:, None])

    nt = (((1,), (1,)), ((), ()))
    tn = (((0,), (0,)), ((), ()))
    scores = lax.dot_general(queries, keys, nt, preferred_element_type=F32) * scale
    scores = jnp.where(allowed, scores, NEG)
    row_max = jnp.max(scores, axis=1, keepdims=True)
    weights = jnp.where(allowed, jnp.exp(scores - row_max), 0.0)
    row_sum = jnp.sum(weights, axis=1, keepdims=True)
    attention = (jnp.dot(weights.astype(BF16), values, preferred_element_type=F32) / row_sum).astype(
        BF16
    )
    attn_mine, attn_other = gather_row(attention)
    layer_out = scatter_sum_col(attn_mine, attn_other, w_out_rel.T, core)

    row_delta = jnp.sum(grad_rows.astype(F32) * attention.astype(F32), axis=1, keepdims=True)
    probs = jnp.where(allowed, jnp.exp(scores - (row_max + jnp.log(row_sum))), 0.0)
    grad_probs = lax.dot_general(grad_rows, values, nt, preferred_element_type=F32)
    grad_scores = (probs * (grad_probs - row_delta)).astype(BF16)
    grad_query = jnp.dot(grad_scores, keys, preferred_element_type=F32) * scale
    grad_key = lax.dot_general(grad_scores, queries, tn, preferred_element_type=F32) * scale
    grad_value = lax.dot_general(probs.astype(BF16), grad_rows, tn, preferred_element_type=F32)
    half = queries.shape[0]
    grad_kv = jnp.concatenate([grad_key, grad_value], axis=1)
    grad_kv = grad_kv[:half] + swap_cores(grad_kv[half:].astype(BF16)).astype(F32)
    grads = jnp.concatenate([grad_query, grad_kv], axis=1).astype(BF16)
    g_mine, g_other = gather_row(grads)
    grad_x = scatter_sum_col(g_mine, g_other, w_rel, core)

    x_all = jnp.concatenate([x_mine, x_other], axis=0)
    g_all = jnp.concatenate([g_mine, g_other], axis=0)
    back = (RING - z_id) % RING
    g_abs = turned([g_all[:, i * 3 * HD : (i + 1) * 3 * HD] for i in range(RING)], back)
    g_abs = g_abs.reshape(RING, -1, 3, HD)
    grad_qkv = jnp.einsum("tk,htcn->ckhn", x_all, g_abs, preferred_element_type=F32)
    grad_qkv = grad_qkv.reshape(3, features, RING * HD)

    attn_all = jnp.concatenate([attn_mine, attn_other], axis=0)
    attn_abs = turned([attn_all[:, i * HD : (i + 1) * HD] for i in range(RING)], back)
    dy_all = jnp.concatenate([dy_mine, dy_other], axis=0)
    grad_out = jnp.einsum("htn,td->hnd", attn_abs, dy_all, preferred_element_type=F32)
    grad_out = grad_out.reshape(RING * HD, features)
    return (layer_out, grad_x, grad_qkv, grad_out)


def solution(mesh):
    in_specs = (P("col", "row"), P(None, "row", "col"), P("col", "row"), P(), P("col", "row"))
    out_specs = (P("col", "row"), P("col", "row"), P(None, "row", "col"), P("col", "row"))
    return jax.shard_map(
        on_device, mesh=mesh, in_specs=in_specs, out_specs=out_specs, check_vma=False
    )
```

```python
import math

import jax
import jax.numpy as jnp
from jax import lax
from jax.experimental import pallas as pl
from jax.experimental.pallas import tpu as pltpu
from jax.sharding import PartitionSpec as P

HD = 128
BLOCK = 128
NEG = -1e30
F32 = jnp.float32
BF16 = jnp.bfloat16
NT = (((1,), (1,)), ((), ()))
TN = (((0,), (0,)), ((), ()))
MIB = 1024 * 1024

RING = 4
CORES = 2
QKV = 3


def to_x(value, step):
    pairs = [(c, (c // RING + step) % RING * RING + c % RING) for c in range(RING * RING)]
    return lax.ppermute(value, "col", pairs)


def to_y(value, step):
    pairs = [(c, c // RING * RING + (c % RING + step) % RING) for c in range(RING * RING)]
    return lax.ppermute(value, "col", pairs)


def to_z(value, step):
    pairs = [(r, (r // CORES + step) % RING * CORES + r % CORES) for r in range(RING * CORES)]
    return lax.ppermute(value, "row", pairs)


def swap_cores(value):
    pairs = [(r, r // CORES * CORES + 1 - r % CORES) for r in range(RING * CORES)]
    return lax.ppermute(value, "row", pairs)


def tied(values, others):
    out = lax.optimization_barrier((tuple(values), tuple(others)))
    return list(out[0])


def mm(a, b):
    return jnp.dot(a, b, preferred_element_type=F32)


def whole(array):
    return pl.BlockSpec(array.shape, lambda i, s: (0,) * array.ndim)


def shape_of(array_shape, dtype):
    return jax.ShapeDtypeStruct(array_shape, dtype)


def call(
    kernel,
    scalar,
    inputs,
    in_specs,
    out_shape,
    out_specs,
    grid=1,
    flops=0,
    moved=0,
    scratch=(),
    limit=16,
):
    return pl.pallas_call(
        kernel,
        grid_spec=pltpu.PrefetchScalarGridSpec(
            num_scalar_prefetch=1,
            grid=(grid,),
            in_specs=in_specs,
            out_specs=out_specs,
            scratch_shapes=list(scratch),
        ),
        out_shape=out_shape,
        compiler_params=pltpu.CompilerParams(vmem_limit_bytes=limit * MIB),
        cost_estimate=pl.CostEstimate(flops=flops, bytes_accessed=moved, transcendentals=0),
    )(scalar, *inputs)


def turn_weights(z_arg, w_qkv):
    count, depth, width = w_qkv.shape

    def kernel(z_ref, w_ref, out_ref):
        for which in range(count):
            out_ref[which * HD : (which + 1) * HD, :] = w_ref[which].T

    return call(
        kernel,
        z_arg,
        [w_qkv],
        [pl.BlockSpec((count, depth, HD), lambda d, z: (0, 0, (z[0] + d) % RING))],
        shape_of((count * width, depth), BF16),
        pl.BlockSpec((count * HD, depth), lambda d, z: (d, 0)),
        grid=RING,
        moved=4 * count * depth * width,
    )


def stack_blocks(core_arg, blocks):
    rows, width = blocks[0].shape
    half = rows // 2

    def kernel(core_ref, *refs):
        out_ref = refs[RING]
        for side in range(2):
            start = pl.multiple_of((core_ref[0] ^ side) * half, half)
            for i in range(RING):
                place = (side * RING + i) * half
                out_ref[place : place + half, :] = refs[i][pl.ds(start, half), :]

    out = shape_of((RING * rows, width), BF16)
    return call(
        kernel, core_arg, blocks, [whole(b) for b in blocks], out, whole(out), moved=8 * rows * width * 2
    )


def ring_gather(block, send):
    half = block.shape[0] // 2
    before, after = send(block, 1), send(block, -1)
    far = (send(before[:half], 1), send(after[half:], -1))
    return [block, after, far, before]


def near_gather(block, send):
    return [block] + [send(block, -step) for step in range(1, RING)]


def halves(parts, side, width=None, column=lambda i: 0):
    arrays, specs = [], []
    for part in parts:
        array, place = (part[side], 0) if isinstance(part, tuple) else (part, side)
        rows = array.shape[0] if isinstance(part, tuple) else array.shape[0] // 2
        arrays.append(array)
        specs.append(
            pl.BlockSpec(
                (rows, width or array.shape[1]), lambda i, s, place=place: (place, column(i))
            )
        )
    return arrays, specs


def flat(parts):
    return [array for part in parts for array in (part if isinstance(part, tuple) else (part,))]


def joined(parts, refs):
    values, refs = [], list(refs)
    for part in parts:
        if isinstance(part, tuple):
            values.append(jnp.concatenate([refs.pop(0)[...] for _ in part], axis=0))
        else:
            values.append(refs.pop(0)[...])
    return values


def by_place(refs, rows):
    return jnp.concatenate(
        [refs[dx][dy * rows : (dy + 1) * rows, :] for dy in range(RING) for dx in range(RING)], axis=0
    )


def head_products(z_arg, x_parts, dy_parts, w_qkv, w_out, side, dtype):
    count, depth, _ = w_qkv.shape
    x_arrays, x_specs = halves(x_parts, side)
    dy_arrays, dy_specs = halves(dy_parts, side)
    part = dy_specs[0].block_shape[0] // RING
    tokens = part * RING * RING
    width = (count + 1) * HD

    def kernel(z_ref, *refs):
        x_refs, dy_refs, (w_ref, wo_ref) = refs[:RING], refs[RING : 2 * RING], refs[2 * RING : 2 * RING + 2]
        out_refs, (x_all, dy_all) = refs[2 * RING + 2 : -2], refs[-2:]
        step = pl.program_id(0)

        @pl.when(step == 0)
        def _():
            x_all[...] = jnp.concatenate([ref[...] for ref in x_refs], axis=0)
            dy_all[...] = by_place(dy_refs, part)

        w = jnp.concatenate([w_ref[which] for which in range(count)], axis=1)
        prod = mm(x_all[...], w).astype(dtype)
        prod_out = lax.dot_general(
            dy_all[...], wo_ref[...], NT, preferred_element_type=F32
        ).astype(dtype)
        for i, out_ref in enumerate(out_refs):

            @pl.when(step == i)
            def _():
                out_ref[:, : count * HD] = prod
                out_ref[:, count * HD :] = prod_out

    outs = [shape_of((tokens, width), dtype) for _ in range(RING)]
    return call(
        kernel,
        z_arg,
        x_arrays + dy_arrays + [w_qkv, w_out],
        x_specs
        + dy_specs
        + [
            pl.BlockSpec((count, depth, HD), lambda i, z: (0, 0, (z[0] + i) % RING)),
            pl.BlockSpec((HD, depth), lambda i, z: ((z[0] + i) % RING, 0)),
        ],
        outs,
        [whole(o) for o in outs],
        grid=RING,
        flops=2 * tokens * depth * width * RING,
        moved=8 * MIB,
        scratch=[pltpu.VMEM((tokens, depth), BF16), pltpu.VMEM((tokens, depth), BF16)],
    )


def small(kernel, scalar, inputs, outs):
    moved = sum(a.size * a.dtype.itemsize for a in list(inputs) + list(outs))
    return call(
        kernel, scalar, inputs, [whole(a) for a in inputs], outs, [whole(o) for o in outs], moved=moved
    )


def first_pieces(scalar, own, got):
    half, width = own.shape[0] // 2, own.shape[1]

    def kernel(s_ref, own_ref, got_ref, top_ref, low_ref):
        total = (own_ref[...] + got_ref[...].astype(F32)).astype(BF16)
        top_ref[...] = total[:half]
        low_ref[...] = total[half:]

    return small(kernel, scalar, [own, got], [shape_of((half, width), BF16)] * 2)


def second_pieces(scalar, one, got_one, top, three, got_three, low):
    half = top.shape[0]

    def kernel(s_ref, one_ref, got_one_ref, top_ref, three_ref, got_three_ref, low_ref, out1, out3):
        first = one_ref[...] + got_one_ref[...].astype(F32)
        out1[:half, :] = (first[:half] + top_ref[...].astype(F32)).astype(BF16)
        out1[half:, :] = first[half:].astype(BF16)
        second = three_ref[...] + got_three_ref[...].astype(F32)
        out3[:half, :] = second[:half].astype(BF16)
        out3[half:, :] = (second[half:] + low_ref[...].astype(F32)).astype(BF16)

    inputs = [one, got_one, top, three, got_three, low]
    return small(kernel, scalar, inputs, [shape_of(one.shape, BF16)] * 2)


def own_piece(scalar, own, got, one, three):
    def kernel(s_ref, own_ref, got_ref, one_ref, three_ref, out_ref, kv_ref):
        total = own_ref[...] + got_ref[...].astype(F32)
        total = total + one_ref[...].astype(F32) + three_ref[...].astype(F32)
        total = total.astype(BF16)
        out_ref[...] = total
        kv_ref[...] = total[:, HD : 3 * HD]

    outs = [shape_of(own.shape, BF16), shape_of((own.shape[0], 2 * HD), BF16)]
    return small(kernel, scalar, [own, got, one, three], outs)


def project(z_arg, x_parts, dy_parts, w_qkv, w_out):
    sent = head_products(z_arg, x_parts, dy_parts, w_qkv, w_out, 1, BF16)
    got = {step: swap_cores(sent[step]) for step in (2, 1, 3, 0)}
    own = head_products(z_arg, x_parts, dy_parts, w_qkv, w_out, 0, F32)
    top, low = first_pieces(z_arg, own[2], got[2])
    top, low = to_z(top, 1), to_z(low, -1)
    one, three = second_pieces(z_arg, own[1], got[1], top, own[3], got[3], low)
    x_late = tied(flat(x_parts) + flat(dy_parts), [one, three])
    one, three = to_z(one, 1), to_z(three, -1)
    both, kv = own_piece(z_arg, own[0], got[0], one, three)
    return both, kv, x_late


def arrange(scalar, x_parts, dy_parts):
    features = x_parts[0].shape[1]
    tokens = 4 * x_parts[0].shape[0]
    tile = 256
    arrays, specs = [], []
    for parts in (x_parts, dy_parts):
        for side in range(2):
            side_arrays, side_specs = halves(parts, side, tile, lambda i: i)
            arrays += side_arrays
            specs += side_specs
    part = specs[0].block_shape[0] // RING

    def kernel(s_ref, *refs):
        x_t_ref, dy_ref = refs[4 * RING :]
        x = jnp.concatenate([ref[...] for ref in refs[: 2 * RING]], axis=0)
        x_t_ref[...] = x.T
        for side in range(2):
            group = refs[(2 + side) * RING : (3 + side) * RING]
            dy_ref[side * tokens // 2 : (side + 1) * tokens // 2, :] = by_place(group, part)

    return call(
        kernel,
        scalar,
        arrays,
        specs,
        [shape_of((features, tokens), BF16), shape_of((tokens, features), BF16)],
        [
            pl.BlockSpec((tile, tokens), lambda i, s: (i, 0)),
            pl.BlockSpec((tokens, tile), lambda i, s: (0, i)),
        ],
        grid=features // tile,
        moved=8 * tokens * features,
    )


def attend(scalar, both, kv_other, tok_col):
    tokens = both.shape[0]
    scale = 1.0 / math.sqrt(HD)
    tile = 128
    part = tok_col // 2

    def kernel(s_ref, both_ref, other_ref, query_out, attn_out, own_out, other_out, probs_all, grads_all):
        def position(index, half):
            dy, dx, token = index // (RING * part), index // part % RING, index % part
            device = (s_ref[0] + dx) % RING * RING + (s_ref[1] + dy) % RING
            return device * tok_col + half * part + token

        side = s_ref[2]
        key_index = lax.broadcasted_iota(jnp.int32, (1, 2 * tokens), 1)
        key_pos = position(key_index % tokens, side ^ (key_index // tokens))
        keys = jnp.concatenate([both_ref[:, HD : 2 * HD], other_ref[:, :HD]], axis=0)
        values = jnp.concatenate([both_ref[:, 2 * HD : 3 * HD], other_ref[:, HD:]], axis=0)
        for start in range(0, tokens, tile):
            rows = slice(start, start + tile)
            queries, grad_rows = both_ref[rows, :HD], both_ref[rows, 3 * HD :]
            query_index = start + lax.broadcasted_iota(jnp.int32, (tile, 1), 0)
            query_pos = position(query_index, side)
            first_pos = jnp.zeros_like(query_pos)
            for block in range(s_ref.shape[0] - 3):
                first_pos = jnp.where(query_pos // BLOCK == block, s_ref[3 + block], first_pos)
            allowed = (key_pos >= first_pos) & (key_pos <= query_pos)
            scores = lax.dot_general(queries, keys, NT, preferred_element_type=F32) * scale
            scores = jnp.where(allowed, scores, NEG)
            row_max = jnp.max(scores, axis=1, keepdims=True)
            weights = jnp.where(allowed, jnp.exp(scores - row_max), 0.0)
            row_sum = jnp.sum(weights, axis=1, keepdims=True)
            attention = (mm(weights.astype(BF16), values) / row_sum).astype(BF16)
            attn_out[rows, :] = attention
            row_delta = jnp.sum(
                grad_rows.astype(F32) * attention.astype(F32), axis=1, keepdims=True
            )
            probs = weights * (1.0 / row_sum)
            grad_probs = lax.dot_general(grad_rows, values, NT, preferred_element_type=F32)
            grad_scores = (probs * (grad_probs - row_delta)).astype(BF16)
            query_out[rows, :] = (mm(grad_scores, keys) * scale).astype(BF16)
            probs_all[rows, :] = probs.astype(BF16)
            grads_all[rows, :] = grad_scores
        grad_keys = (
            lax.dot_general(grads_all[...], both_ref[:, :HD], TN, preferred_element_type=F32) * scale
        )
        grad_values = lax.dot_general(
            probs_all[...], both_ref[:, 3 * HD :], TN, preferred_element_type=F32
        )
        own_out[:, :HD] = grad_keys[:tokens]
        own_out[:, HD:] = grad_values[:tokens]
        other_out[:, :HD] = grad_keys[tokens:].astype(BF16)
        other_out[:, HD:] = grad_values[tokens:].astype(BF16)

    outs = [
        shape_of((tokens, HD), BF16),
        shape_of((tokens, HD), BF16),
        shape_of((tokens, 2 * HD), F32),
        shape_of((tokens, 2 * HD), BF16),
    ]
    return call(
        kernel,
        scalar,
        [both, kv_other],
        [whole(both), whole(kv_other)],
        outs,
        [whole(o) for o in outs],
        flops=14 * tokens * 2 * tokens * HD,
        moved=4 * MIB,
        scratch=[pltpu.VMEM((tokens, 2 * tokens), BF16), pltpu.VMEM((tokens, 2 * tokens), BF16)],
    )


def pack_grads(scalar, grad_query, own, got, attention):
    def kernel(s_ref, query_ref, own_ref, got_ref, attn_ref, out_ref):
        out_ref[:, :HD] = query_ref[...]
        out_ref[:, HD : 3 * HD] = (own_ref[...] + got_ref[...].astype(F32)).astype(BF16)
        out_ref[:, 3 * HD :] = attn_ref[...]

    inputs = [grad_query, own, got, attention]
    (out,) = small(kernel, scalar, inputs, [shape_of((grad_query.shape[0], 4 * HD), BF16)])
    return out


def piece_y(scalar, mine, other, weights, step, received, dtype, cut):
    rows = mine[0].shape[0] // RING
    width = QKV * HD
    depth, features = weights.shape
    arrays, specs = [], []
    for part in mine + other:
        if isinstance(part, tuple):
            count = part[0].shape[0] // rows
            array, place = part[step // count], step % count
        else:
            array, place = part, step
        arrays.append(array)
        specs.append(pl.BlockSpec((rows, width), lambda i, s, place=place: (place, 0)))

    def kernel(s_ref, *refs):
        top = jnp.concatenate([ref[...] for ref in refs[:RING]], axis=1)
        low = jnp.concatenate([ref[...] for ref in refs[RING : 2 * RING]], axis=1)
        prod = mm(jnp.concatenate([top, low], axis=0), refs[2 * RING][...])
        finish_piece(prod, refs[2 * RING + 1 :], step, received, dtype, cut)

    return piece_call(
        kernel,
        scalar,
        arrays + [weights],
        specs + [whole(weights)],
        (2 * rows, features),
        depth,
        received,
        dtype,
        cut,
    )


def finish_piece(prod, refs, step, received, dtype, cut):
    half = prod.shape[0] // 2
    top, low = prod[:half], prod[half:]
    if received:
        if step == 1:
            top = top + refs[0][...].astype(F32)
        else:
            low = low + refs[0][...].astype(F32)
    outs = refs[len(received) :]
    if cut:
        outs[0][...] = top.astype(dtype)
        outs[1][...] = low.astype(dtype)
    else:
        outs[0][:half, :] = top.astype(dtype)
        outs[0][half:, :] = low.astype(dtype)


def piece_call(kernel, scalar, inputs, specs, shape, depth, received, dtype, cut):
    rows, features = shape
    outs = [shape_of((rows // 2, features), dtype)] * 2 if cut else [shape_of(shape, dtype)]
    return call(
        kernel,
        scalar,
        inputs + received,
        specs + [whole(r) for r in received],
        outs,
        [whole(o) for o in outs],
        flops=2 * rows * depth * features,
        moved=2 * depth * (rows + features),
    )


def piece_x(z_arg, mine, other, w_out, step, received, dtype, cut):
    rows = mine[0].shape[0] // (RING * RING)
    depth, features = w_out.shape

    arrays = flat(mine) + flat(other)
    count = len(arrays) // 2

    def kernel(z_ref, *refs):
        def taken(parts, group):
            return jnp.concatenate(
                [
                    jnp.concatenate(
                        [
                            value[(dy * RING + step) * rows : (dy * RING + step + 1) * rows]
                            for dy in range(RING)
                        ],
                        axis=0,
                    )
                    for value in joined(parts, group)
                ],
                axis=1,
            )

        both = jnp.concatenate(
            [taken(mine, refs[:count]), taken(other, refs[count : 2 * count])], axis=0
        )
        w = jnp.concatenate([ref[...] for ref in refs[2 * count : 2 * count + RING]], axis=0)
        finish_piece(mm(both, w), refs[2 * count + RING :], step, received, dtype, cut)

    specs = [pl.BlockSpec((a.shape[0], HD), lambda i, z: (0, QKV)) for a in arrays]
    w_specs = [
        pl.BlockSpec((HD, features), lambda i, z, d=d: ((z[0] + d) % RING, 0)) for d in range(RING)
    ]
    return piece_call(
        kernel,
        z_arg,
        arrays + [w_out] * RING,
        specs + w_specs,
        (2 * rows * RING, features),
        depth,
        received,
        dtype,
        cut,
    )


def split_sum(scalar, own, arrived):
    rows, width = own.shape
    part = rows // (2 * RING)

    def kernel(s_ref, own_ref, *refs):
        outs = refs[len(arrived) :]
        for i, out_ref in enumerate(outs):
            for side in range(2):
                place = pl.ds((side * RING + i) * part, part)
                total = own_ref[place, :]
                for ref in refs[: len(arrived)]:
                    total = total + ref[place, :].astype(F32)
                out_ref[side * part : (side + 1) * part, :] = total.astype(out_ref.dtype)

    outs = [shape_of((2 * part, width), BF16 if i else F32) for i in range(RING)]
    inputs = [own] + arrived
    return call(
        kernel,
        scalar,
        inputs,
        [whole(a) for a in inputs],
        outs,
        [whole(o) for o in outs],
        moved=14 * rows * width,
    )


def last_sum(core_arg, own, arrived):
    rows, width = own.shape
    half = rows // 2

    def kernel(core_ref, own_ref, *refs):
        out_ref = refs[len(arrived)]
        total = own_ref[...]
        for ref in refs[: len(arrived)]:
            total = total + ref[...].astype(F32)
        for side in range(2):
            start = pl.multiple_of((core_ref[0] ^ side) * half, half)
            out_ref[pl.ds(start, half), :] = total[side * half : (side + 1) * half].astype(BF16)

    out = shape_of((rows, width), BF16)
    inputs = [own] + arrived
    return call(
        kernel, core_arg, inputs, [whole(a) for a in inputs], out, whole(out), moved=14 * rows * width
    )


def scatter_sum_col(z_arg, core_arg, mine, other, weights, piece, first, second):
    def product(step, received, dtype, cut=False):
        return piece(z_arg, mine, other, weights, step, received, dtype, cut)

    top, low = product(2, [], BF16, cut=True)
    top, low = first(top, 1), first(low, -1)
    (one,) = product(1, [top], BF16)
    one = first(one, 1)
    (three,) = product(3, [low], BF16)
    three = first(three, -1)
    (own,) = product(0, [], F32)
    own, *parts = split_sum(z_arg, own, [one, three])
    return last_sum(core_arg, own, [second(parts[step - 1], step) for step in (2, 1, 3)])


def grad_qkv_product(z_arg, x_t, g_mine, g_other):
    features, tokens = x_t.shape
    tile = 256
    width = QKV * HD
    g_arrays = flat(g_mine) + flat(g_other)

    def kernel(z_ref, x_ref, *refs):
        g_refs, out_ref = refs[:-1], refs[-1]
        mine = joined(g_mine, g_refs[: len(g_refs) // 2])
        other = joined(g_other, g_refs[len(g_refs) // 2 :])
        for first in range(0, RING, 2):
            g = jnp.concatenate(
                [
                    jnp.concatenate([group[first], group[first + 1]], axis=1)
                    for group in (mine, other)
                ],
                axis=0,
            )
            prod = mm(x_ref[...], g)
            for step in range(2):
                head = lax.rem(z_ref[0] + first + step, RING)
                place = pl.ds(pl.multiple_of(head * HD, HD), HD)
                for which in range(QKV):
                    start = step * width + which * HD
                    out_ref[which, :, place] = prod[:, start : start + HD]

    return call(
        kernel,
        z_arg,
        [x_t] + g_arrays,
        [pl.BlockSpec((tile, tokens), lambda i, z: (i, 0))]
        + [pl.BlockSpec((g.shape[0], width), lambda i, z: (0, 0)) for g in g_arrays],
        shape_of((QKV, features, RING * HD), F32),
        pl.BlockSpec((QKV, tile, RING * HD), lambda i, z: (0, i, 0)),
        grid=features // tile,
        flops=2 * tokens * features * RING * width,
        moved=12 * MIB,
    )


def grad_out_product(z_arg, g_mine, g_other, dy_all):
    tokens, features = dy_all.shape
    tile = 512
    g_arrays = flat(g_mine) + flat(g_other)

    def kernel(z_ref, *refs):
        g_refs, dy_ref, out_ref = refs[:-2], refs[-2], refs[-1]
        attn = jnp.concatenate(
            [
                jnp.concatenate(joined(parts, group), axis=1)
                for parts, group in (
                    (g_mine, g_refs[: len(g_refs) // 2]),
                    (g_other, g_refs[len(g_refs) // 2 :]),
                )
            ],
            axis=0,
        )
        prod = lax.dot_general(attn, dy_ref[...], TN, preferred_element_type=F32)
        for step in range(RING):
            head = lax.rem(z_ref[0] + step, RING)
            out_ref[pl.ds(pl.multiple_of(head * HD, HD), HD), :] = prod[step * HD : (step + 1) * HD]

    return call(
        kernel,
        z_arg,
        g_arrays + [dy_all],
        [pl.BlockSpec((g.shape[0], HD), lambda i, z: (0, QKV)) for g in g_arrays]
        + [pl.BlockSpec((tokens, tile), lambda i, z: (0, i))],
        shape_of((RING * HD, features), F32),
        pl.BlockSpec((RING * HD, tile), lambda i, z: (0, i)),
        grid=features // tile,
        flops=2 * tokens * features * RING * HD,
        moved=5 * MIB,
    )


def on_device(normed, w_qkv, w_out, doc_start, grad_y):
    row_id, col_id = lax.axis_index("row"), lax.axis_index("col")
    z_id, core = row_id // CORES, row_id % CORES
    x_id, y_id = col_id // RING, col_id % RING
    z_arg, core_arg = z_id.reshape(1), core.reshape(1)
    place_arg = jnp.concatenate([jnp.stack([x_id, y_id, core]), doc_start])

    x_blocks, dy_blocks = near_gather(normed, to_x), near_gather(grad_y, to_y)
    blocks = tied(x_blocks + dy_blocks, [])
    x_parts = ring_gather(stack_blocks(core_arg, blocks[:RING]), to_y)
    dy_parts = ring_gather(stack_blocks(core_arg, blocks[RING:]), to_x)
    (w_turn,) = tied([w_qkv], [x_parts[1]])
    w_rel_t = turn_weights(z_arg, w_turn)
    flat_parts = tied(flat(x_parts) + flat(dy_parts), [w_rel_t])

    def parts_of(arrays):
        count = len(arrays) // 2
        return [[a[0], a[1], (a[2], a[3]), a[4]] for a in (arrays[:count], arrays[count:])]

    x_parts, dy_parts = parts_of(flat_parts)
    both, kv_mine, late = project(z_arg, x_parts, dy_parts, w_qkv, w_out)
    x_t, dy_all = arrange(z_arg, *parts_of(late))

    grad_query, attention, grad_kv, grad_kv_other = attend(
        place_arg, both, swap_cores(kv_mine), normed.shape[0]
    )
    grads = pack_grads(z_arg, grad_query, grad_kv, swap_cores(grad_kv_other), attention)
    g_mine = ring_gather(grads, to_z)
    g_other = [
        tuple(swap_cores(p) for p in part) if isinstance(part, tuple) else swap_cores(part)
        for part in g_mine
    ]

    layer_out = scatter_sum_col(z_arg, core_arg, g_mine, g_other, w_out, piece_x, to_x, to_y)
    grad_x = scatter_sum_col(z_arg, core_arg, g_mine, g_other, w_rel_t, piece_y, to_y, to_x)
    grad_qkv = grad_qkv_product(z_arg, x_t, g_mine, g_other)
    grad_out = grad_out_product(z_arg, g_mine, g_other, dy_all)
    return (layer_out, grad_x, grad_qkv, grad_out)


def solution(mesh):
    in_specs = (P("col", "row"), P(None, "row", "col"), P("col", "row"), P(), P("col", "row"))
    out_specs = (P("col", "row"), P("col", "row"), P(None, "row", "col"), P("col", "row"))
    return jax.shard_map(
        on_device, mesh=mesh, in_specs=in_specs, out_specs=out_specs, check_vma=False
    )
```

```python
import math

import jax
import jax.numpy as jnp
from jax import lax
from jax.experimental import pallas as pl
from jax.experimental.pallas import tpu as pltpu
from jax.sharding import PartitionSpec as P

HD = 128
BLOCK = 128
NEG = -1e30
F32 = jnp.float32
BF16 = jnp.bfloat16
NT = (((1,), (1,)), ((), ()))
TN = (((0,), (0,)), ((), ()))
MIB = 1024 * 1024

RING = 4
CORES = 2
QKV = 3


def to_x(value, step):
    pairs = [(c, (c // RING + step) % RING * RING + c % RING) for c in range(RING * RING)]
    return lax.ppermute(value, "col", pairs)


def to_y(value, step):
    pairs = [(c, c // RING * RING + (c % RING + step) % RING) for c in range(RING * RING)]
    return lax.ppermute(value, "col", pairs)


def to_z(value, step):
    pairs = [(r, (r // CORES + step) % RING * CORES + r % CORES) for r in range(RING * CORES)]
    return lax.ppermute(value, "row", pairs)


def swap_cores(value):
    pairs = [(r, r // CORES * CORES + 1 - r % CORES) for r in range(RING * CORES)]
    return lax.ppermute(value, "row", pairs)


def tied(values, others):
    out = lax.optimization_barrier((tuple(values), tuple(others)))
    return list(out[0])


def mm(a, b):
    return jnp.dot(a, b, preferred_element_type=F32)


def whole(array):
    return pl.BlockSpec(array.shape, lambda i, s: (0,) * array.ndim)


def shape_of(array_shape, dtype):
    return jax.ShapeDtypeStruct(array_shape, dtype)


def call(
    kernel,
    scalar,
    inputs,
    in_specs,
    out_shape,
    out_specs,
    grid=1,
    flops=0,
    moved=0,
    scratch=(),
    limit=16,
    after=(),
):
    count = len(inputs)

    def wrapped(scalar_ref, *refs):
        kernel(scalar_ref, *refs[:count], *refs[count + len(after) :])

    inputs = list(inputs) + list(after)
    in_specs = list(in_specs) + [pl.BlockSpec(memory_space=pl.ANY)] * len(after)
    return pl.pallas_call(
        wrapped,
        grid_spec=pltpu.PrefetchScalarGridSpec(
            num_scalar_prefetch=1,
            grid=(grid,),
            in_specs=in_specs,
            out_specs=out_specs,
            scratch_shapes=list(scratch),
        ),
        out_shape=out_shape,
        compiler_params=pltpu.CompilerParams(vmem_limit_bytes=limit * MIB),
        cost_estimate=pl.CostEstimate(flops=flops, bytes_accessed=moved, transcendentals=0),
    )(scalar, *inputs)


def turn_weights(z_arg, w_qkv):
    count, depth, width = w_qkv.shape

    def kernel(z_ref, w_ref, out_ref):
        for which in range(count):
            out_ref[which * HD : (which + 1) * HD, :] = w_ref[which].T

    return call(
        kernel,
        z_arg,
        [w_qkv],
        [pl.BlockSpec((count, depth, HD), lambda d, z: (0, 0, (z[0] + d) % RING))],
        shape_of((count * width, depth), BF16),
        pl.BlockSpec((count * HD, depth), lambda d, z: (d, 0)),
        grid=RING,
        moved=4 * count * depth * width,
    )


def stack_blocks(core_arg, blocks):
    rows, width = blocks[0].shape
    half = rows // 2

    def kernel(core_ref, *refs):
        out_ref = refs[RING]
        for side in range(2):
            start = pl.multiple_of((core_ref[0] ^ side) * half, half)
            for i in range(RING):
                place = (side * RING + i) * half
                out_ref[place : place + half, :] = refs[i][pl.ds(start, half), :]

    out = shape_of((RING * rows, width), BF16)
    return call(
        kernel, core_arg, blocks, [whole(b) for b in blocks], out, whole(out), moved=8 * rows * width * 2
    )


def ring_gather(block, send):
    half = block.shape[0] // 2
    before, after = send(block, 1), send(block, -1)
    far = (send(before[:half], 1), send(after[half:], -1))
    return [block, after, far, before]


def near_gather(block, send):
    return [block] + [send(block, -step) for step in range(1, RING)]


def halves(parts, side, width=None, column=lambda i: 0):
    arrays, specs = [], []
    for part in parts:
        array, place = (part[side], 0) if isinstance(part, tuple) else (part, side)
        rows = array.shape[0] if isinstance(part, tuple) else array.shape[0] // 2
        arrays.append(array)
        specs.append(
            pl.BlockSpec(
                (rows, width or array.shape[1]), lambda i, s, place=place: (place, column(i))
            )
        )
    return arrays, specs


def flat(parts):
    return [array for part in parts for array in (part if isinstance(part, tuple) else (part,))]


def joined(parts, refs):
    values, refs = [], list(refs)
    for part in parts:
        if isinstance(part, tuple):
            values.append(jnp.concatenate([refs.pop(0)[...] for _ in part], axis=0))
        else:
            values.append(refs.pop(0)[...])
    return values


def by_place(refs, rows):
    return jnp.concatenate(
        [refs[dx][dy * rows : (dy + 1) * rows, :] for dy in range(RING) for dx in range(RING)], axis=0
    )


def head_products(z_arg, x_parts, dy_parts, w_qkv, w_out, side, dtype):
    count, depth, _ = w_qkv.shape
    x_arrays, x_specs = halves(x_parts, side)
    dy_arrays, dy_specs = halves(dy_parts, side)
    part = dy_specs[0].block_shape[0] // RING
    tokens = part * RING * RING
    width = (count + 1) * HD

    def kernel(z_ref, *refs):
        x_refs, dy_refs, (w_ref, wo_ref) = refs[:RING], refs[RING : 2 * RING], refs[2 * RING : 2 * RING + 2]
        out_refs = refs[2 * RING + 2 :]
        x = jnp.concatenate([ref[...] for ref in x_refs], axis=0)
        dy = by_place(dy_refs, part)
        places = [
            pl.ds(pl.multiple_of(lax.rem(z_ref[0] + step, RING) * HD, HD), HD) for step in range(RING)
        ]
        for pair in ((2, 1), (3, 0)):
            w = jnp.concatenate(
                [w_ref[which, :, places[step]] for step in pair for which in range(count)], axis=1
            )
            wo = jnp.concatenate([wo_ref[places[step], :] for step in pair], axis=0)
            prod = mm(x, w)
            prod_out = lax.dot_general(dy, wo, NT, preferred_element_type=F32)
            for i, step in enumerate(pair):
                out_refs[step][:, : count * HD] = prod[
                    :, i * count * HD : (i + 1) * count * HD
                ].astype(dtype)
                out_refs[step][:, count * HD :] = prod_out[:, i * HD : (i + 1) * HD].astype(dtype)

    outs = [shape_of((tokens, width), dtype) for _ in range(RING)]
    return call(
        kernel,
        z_arg,
        x_arrays + dy_arrays + [w_qkv, w_out],
        x_specs + dy_specs + [whole(w_qkv), whole(w_out)],
        outs,
        [whole(o) for o in outs],
        flops=2 * tokens * depth * width * RING,
        moved=8 * MIB,
        limit=24,
    )


def small(kernel, scalar, inputs, outs, after=()):
    moved = sum(a.size * a.dtype.itemsize for a in list(inputs) + list(outs))
    return call(
        kernel,
        scalar,
        inputs,
        [whole(a) for a in inputs],
        outs,
        [whole(o) for o in outs],
        moved=moved,
        after=after,
    )


def first_pieces(scalar, own, got):
    half, width = own.shape[0] // 2, own.shape[1]

    def kernel(s_ref, own_ref, got_ref, top_ref, low_ref):
        total = (own_ref[...] + got_ref[...].astype(F32)).astype(BF16)
        top_ref[...] = total[:half]
        low_ref[...] = total[half:]

    return small(kernel, scalar, [own, got], [shape_of((half, width), BF16)] * 2)


def second_pieces(scalar, one, got_one, top, three, got_three, low):
    half = top.shape[0]

    def kernel(s_ref, one_ref, got_one_ref, top_ref, three_ref, got_three_ref, low_ref, out1, out3):
        first = one_ref[...] + got_one_ref[...].astype(F32)
        out1[:half, :] = (first[:half] + top_ref[...].astype(F32)).astype(BF16)
        out1[half:, :] = first[half:].astype(BF16)
        second = three_ref[...] + got_three_ref[...].astype(F32)
        out3[:half, :] = second[:half].astype(BF16)
        out3[half:, :] = (second[half:] + low_ref[...].astype(F32)).astype(BF16)

    inputs = [one, got_one, top, three, got_three, low]
    return small(kernel, scalar, inputs, [shape_of(one.shape, BF16)] * 2)


def own_piece(scalar, own, got, one, three, after):
    def kernel(s_ref, own_ref, got_ref, one_ref, three_ref, out_ref, kv_ref):
        total = own_ref[...] + got_ref[...].astype(F32)
        total = total + one_ref[...].astype(F32) + three_ref[...].astype(F32)
        total = total.astype(BF16)
        out_ref[...] = total
        kv_ref[...] = total[:, HD : 3 * HD]

    outs = [shape_of(own.shape, BF16), shape_of((own.shape[0], 2 * HD), BF16)]
    return small(kernel, scalar, [own, got, one, three], outs, after)


def project(z_arg, x_parts, dy_parts, w_qkv, w_out, meanwhile):
    sent = head_products(z_arg, x_parts, dy_parts, w_qkv, w_out, 1, BF16)
    got = {step: swap_cores(sent[step]) for step in (2, 1, 3, 0)}
    own = head_products(z_arg, x_parts, dy_parts, w_qkv, w_out, 0, F32)
    top, low = first_pieces(z_arg, own[2], got[2])
    top, low = to_z(top, 1), to_z(low, -1)
    one, three = second_pieces(z_arg, own[1], got[1], top, own[3], got[3], low)
    one, three = to_z(one, 1), to_z(three, -1)
    return own_piece(z_arg, own[0], got[0], one, three, meanwhile)


def arrange(scalar, x_parts, dy_parts):
    features = x_parts[0].shape[1]
    tokens = 4 * x_parts[0].shape[0]
    tile = 256
    arrays, specs = [], []
    for parts in (x_parts, dy_parts):
        for side in range(2):
            side_arrays, side_specs = halves(parts, side, tile, lambda i: i)
            arrays += side_arrays
            specs += side_specs
    part = specs[0].block_shape[0] // RING

    def kernel(s_ref, *refs):
        x_t_ref, dy_ref = refs[4 * RING :]
        x = jnp.concatenate([ref[...] for ref in refs[: 2 * RING]], axis=0)
        x_t_ref[...] = x.T
        for side in range(2):
            group = refs[(2 + side) * RING : (3 + side) * RING]
            dy_ref[side * tokens // 2 : (side + 1) * tokens // 2, :] = by_place(group, part)

    return call(
        kernel,
        scalar,
        arrays,
        specs,
        [shape_of((features, tokens), BF16), shape_of((tokens, features), BF16)],
        [
            pl.BlockSpec((tile, tokens), lambda i, s: (i, 0)),
            pl.BlockSpec((tokens, tile), lambda i, s: (0, i)),
        ],
        grid=features // tile,
        moved=8 * tokens * features,
    )


def attend(scalar, both, kv_other, tok_col):
    tokens = both.shape[0]
    scale = 1.0 / math.sqrt(HD)
    tile = 128
    part = tok_col // 2

    def kernel(s_ref, both_ref, other_ref, query_out, attn_out, own_out, other_out, probs_all, grads_all):
        def position(index, half):
            dy, dx, token = index // (RING * part), index // part % RING, index % part
            device = (s_ref[0] + dx) % RING * RING + (s_ref[1] + dy) % RING
            return device * tok_col + half * part + token

        side = s_ref[2]
        key_index = lax.broadcasted_iota(jnp.int32, (1, 2 * tokens), 1)
        key_pos = position(key_index % tokens, side ^ (key_index // tokens))
        keys = jnp.concatenate([both_ref[:, HD : 2 * HD], other_ref[:, :HD]], axis=0)
        values = jnp.concatenate([both_ref[:, 2 * HD : 3 * HD], other_ref[:, HD:]], axis=0)
        for start in range(0, tokens, tile):
            rows = slice(start, start + tile)
            queries, grad_rows = both_ref[rows, :HD], both_ref[rows, 3 * HD :]
            query_index = start + lax.broadcasted_iota(jnp.int32, (tile, 1), 0)
            query_pos = position(query_index, side)
            first_pos = jnp.zeros_like(query_pos)
            for block in range(s_ref.shape[0] - 3):
                first_pos = jnp.where(query_pos // BLOCK == block, s_ref[3 + block], first_pos)
            allowed = (key_pos >= first_pos) & (key_pos <= query_pos)
            scores = lax.dot_general(queries, keys, NT, preferred_element_type=F32) * scale
            scores = jnp.where(allowed, scores, NEG)
            row_max = jnp.max(scores, axis=1, keepdims=True)
            weights = jnp.where(allowed, jnp.exp(scores - row_max), 0.0)
            row_sum = jnp.sum(weights, axis=1, keepdims=True)
            attention = (mm(weights.astype(BF16), values) / row_sum).astype(BF16)
            attn_out[rows, :] = attention
            row_delta = jnp.sum(
                grad_rows.astype(F32) * attention.astype(F32), axis=1, keepdims=True
            )
            probs = weights * (1.0 / row_sum)
            grad_probs = lax.dot_general(grad_rows, values, NT, preferred_element_type=F32)
            grad_scores = (probs * (grad_probs - row_delta)).astype(BF16)
            query_out[rows, :] = (mm(grad_scores, keys) * scale).astype(BF16)
            probs_all[rows, :] = probs.astype(BF16)
            grads_all[rows, :] = grad_scores
        grad_keys = (
            lax.dot_general(grads_all[...], both_ref[:, :HD], TN, preferred_element_type=F32) * scale
        )
        grad_values = lax.dot_general(
            probs_all[...], both_ref[:, 3 * HD :], TN, preferred_element_type=F32
        )
        own_out[:, :HD] = grad_keys[:tokens]
        own_out[:, HD:] = grad_values[:tokens]
        other_out[:, :HD] = grad_keys[tokens:].astype(BF16)
        other_out[:, HD:] = grad_values[tokens:].astype(BF16)

    outs = [
        shape_of((tokens, HD), BF16),
        shape_of((tokens, HD), BF16),
        shape_of((tokens, 2 * HD), F32),
        shape_of((tokens, 2 * HD), BF16),
    ]
    return call(
        kernel,
        scalar,
        [both, kv_other],
        [whole(both), whole(kv_other)],
        outs,
        [whole(o) for o in outs],
        flops=14 * tokens * 2 * tokens * HD,
        moved=4 * MIB,
        scratch=[pltpu.VMEM((tokens, 2 * tokens), BF16), pltpu.VMEM((tokens, 2 * tokens), BF16)],
    )


def pack_grads(scalar, grad_query, own, got, attention):
    def kernel(s_ref, query_ref, own_ref, got_ref, attn_ref, out_ref):
        out_ref[:, :HD] = query_ref[...]
        out_ref[:, HD : 3 * HD] = (own_ref[...] + got_ref[...].astype(F32)).astype(BF16)
        out_ref[:, 3 * HD :] = attn_ref[...]

    inputs = [grad_query, own, got, attention]
    (out,) = small(kernel, scalar, inputs, [shape_of((grad_query.shape[0], 4 * HD), BF16)])
    return out


def piece_y(scalar, mine, other, weights, step, received, dtype, cut, after):
    rows = mine[0].shape[0] // RING
    width = QKV * HD
    depth, features = weights.shape
    arrays, specs = [], []
    for part in mine + other:
        if isinstance(part, tuple):
            count = part[0].shape[0] // rows
            array, place = part[step // count], step % count
        else:
            array, place = part, step
        arrays.append(array)
        specs.append(pl.BlockSpec((rows, width), lambda i, s, place=place: (place, 0)))

    def kernel(s_ref, *refs):
        top = jnp.concatenate([ref[...] for ref in refs[:RING]], axis=1)
        low = jnp.concatenate([ref[...] for ref in refs[RING : 2 * RING]], axis=1)
        prod = mm(jnp.concatenate([top, low], axis=0), refs[2 * RING][...])
        finish_piece(prod, refs[2 * RING + 1 :], step, received, dtype, cut)

    return piece_call(
        kernel,
        scalar,
        arrays + [weights],
        specs + [whole(weights)],
        (2 * rows, features),
        depth,
        received,
        dtype,
        cut,
        after,
    )


def finish_piece(prod, refs, step, received, dtype, cut):
    half = prod.shape[0] // 2
    top, low = prod[:half], prod[half:]
    if received:
        if step == 1:
            top = top + refs[0][...].astype(F32)
        else:
            low = low + refs[0][...].astype(F32)
    outs = refs[len(received) :]
    if cut:
        outs[0][...] = top.astype(dtype)
        outs[1][...] = low.astype(dtype)
    else:
        outs[0][:half, :] = top.astype(dtype)
        outs[0][half:, :] = low.astype(dtype)


def piece_call(kernel, scalar, inputs, specs, shape, depth, received, dtype, cut, after):
    rows, features = shape
    outs = [shape_of((rows // 2, features), dtype)] * 2 if cut else [shape_of(shape, dtype)]
    return call(
        kernel,
        scalar,
        inputs + received,
        specs + [whole(r) for r in received],
        outs,
        [whole(o) for o in outs],
        flops=2 * rows * depth * features,
        moved=2 * depth * (rows + features),
        after=after,
    )


def piece_x(z_arg, mine, other, w_out, step, received, dtype, cut, after):
    rows = mine[0].shape[0] // (RING * RING)
    depth, features = w_out.shape

    arrays = flat(mine) + flat(other)
    count = len(arrays) // 2

    def kernel(z_ref, *refs):
        def taken(parts, group):
            return jnp.concatenate(
                [
                    jnp.concatenate(
                        [
                            value[(dy * RING + step) * rows : (dy * RING + step + 1) * rows]
                            for dy in range(RING)
                        ],
                        axis=0,
                    )
                    for value in joined(parts, group)
                ],
                axis=1,
            )

        both = jnp.concatenate(
            [taken(mine, refs[:count]), taken(other, refs[count : 2 * count])], axis=0
        )
        w = jnp.concatenate([ref[...] for ref in refs[2 * count : 2 * count + RING]], axis=0)
        finish_piece(mm(both, w), refs[2 * count + RING :], step, received, dtype, cut)

    specs = [pl.BlockSpec((a.shape[0], HD), lambda i, z: (0, QKV)) for a in arrays]
    w_specs = [
        pl.BlockSpec((HD, features), lambda i, z, d=d: ((z[0] + d) % RING, 0)) for d in range(RING)
    ]
    return piece_call(
        kernel,
        z_arg,
        arrays + [w_out] * RING,
        specs + w_specs,
        (2 * rows * RING, features),
        depth,
        received,
        dtype,
        cut,
        after,
    )


def split_sum(scalar, own, arrived):
    rows, width = own.shape
    part = rows // (2 * RING)

    def kernel(s_ref, own_ref, *refs):
        outs = refs[len(arrived) :]
        for i, out_ref in enumerate(outs):
            for side in range(2):
                place = pl.ds((side * RING + i) * part, part)
                total = own_ref[place, :]
                for ref in refs[: len(arrived)]:
                    total = total + ref[place, :].astype(F32)
                out_ref[side * part : (side + 1) * part, :] = total.astype(out_ref.dtype)

    outs = [shape_of((2 * part, width), BF16 if i else F32) for i in range(RING)]
    inputs = [own] + arrived
    return call(
        kernel,
        scalar,
        inputs,
        [whole(a) for a in inputs],
        outs,
        [whole(o) for o in outs],
        moved=14 * rows * width,
    )


def last_sum(core_arg, own, arrived):
    rows, width = own.shape
    half = rows // 2

    def kernel(core_ref, own_ref, *refs):
        out_ref = refs[len(arrived)]
        total = own_ref[...]
        for ref in refs[: len(arrived)]:
            total = total + ref[...].astype(F32)
        for side in range(2):
            start = pl.multiple_of((core_ref[0] ^ side) * half, half)
            out_ref[pl.ds(start, half), :] = total[side * half : (side + 1) * half].astype(BF16)

    out = shape_of((rows, width), BF16)
    inputs = [own] + arrived
    return call(
        kernel, core_arg, inputs, [whole(a) for a in inputs], out, whole(out), moved=14 * rows * width
    )


def scatter_sum_col(z_arg, core_arg, mine, other, weights, piece, first, second, after=()):
    def product(step, received, dtype, cut=False, after=()):
        return piece(z_arg, mine, other, weights, step, received, dtype, cut, after)

    top, low = product(2, [], BF16, cut=True)
    top, low = first(top, 1), first(low, -1)
    (one,) = product(1, [top], BF16)
    one = first(one, 1)
    (three,) = product(3, [low], BF16)
    three = first(three, -1)
    (own,) = product(0, [], F32, after=after)
    own, *parts = split_sum(z_arg, own, [one, three])
    return last_sum(core_arg, own, [second(parts[step - 1], step) for step in (2, 1, 3)])


def grad_qkv_product(z_arg, x_t, g_mine, g_other):
    features, tokens = x_t.shape
    tile = 256
    width = QKV * HD
    g_arrays = flat(g_mine) + flat(g_other)

    def kernel(z_ref, x_ref, *refs):
        g_refs, out_ref = refs[:-1], refs[-1]
        mine = joined(g_mine, g_refs[: len(g_refs) // 2])
        other = joined(g_other, g_refs[len(g_refs) // 2 :])
        for first in range(0, RING, 2):
            g = jnp.concatenate(
                [
                    jnp.concatenate([group[first], group[first + 1]], axis=1)
                    for group in (mine, other)
                ],
                axis=0,
            )
            prod = mm(x_ref[...], g)
            for step in range(2):
                head = lax.rem(z_ref[0] + first + step, RING)
                place = pl.ds(pl.multiple_of(head * HD, HD), HD)
                for which in range(QKV):
                    start = step * width + which * HD
                    out_ref[which, :, place] = prod[:, start : start + HD]

    return call(
        kernel,
        z_arg,
        [x_t] + g_arrays,
        [pl.BlockSpec((tile, tokens), lambda i, z: (i, 0))]
        + [pl.BlockSpec((g.shape[0], width), lambda i, z: (0, 0)) for g in g_arrays],
        shape_of((QKV, features, RING * HD), F32),
        pl.BlockSpec((QKV, tile, RING * HD), lambda i, z: (0, i, 0)),
        grid=features // tile,
        flops=2 * tokens * features * RING * width,
        moved=12 * MIB,
    )


def grad_out_product(z_arg, g_mine, g_other, dy_all):
    tokens, features = dy_all.shape
    tile = 512
    g_arrays = flat(g_mine) + flat(g_other)

    def kernel(z_ref, *refs):
        g_refs, dy_ref, out_ref = refs[:-2], refs[-2], refs[-1]
        attn = jnp.concatenate(
            [
                jnp.concatenate(joined(parts, group), axis=1)
                for parts, group in (
                    (g_mine, g_refs[: len(g_refs) // 2]),
                    (g_other, g_refs[len(g_refs) // 2 :]),
                )
            ],
            axis=0,
        )
        prod = lax.dot_general(attn, dy_ref[...], TN, preferred_element_type=F32)
        for step in range(RING):
            head = lax.rem(z_ref[0] + step, RING)
            out_ref[pl.ds(pl.multiple_of(head * HD, HD), HD), :] = prod[step * HD : (step + 1) * HD]

    return call(
        kernel,
        z_arg,
        g_arrays + [dy_all],
        [pl.BlockSpec((g.shape[0], HD), lambda i, z: (0, QKV)) for g in g_arrays]
        + [pl.BlockSpec((tokens, tile), lambda i, z: (0, i))],
        shape_of((RING * HD, features), F32),
        pl.BlockSpec((RING * HD, tile), lambda i, z: (0, i)),
        grid=features // tile,
        flops=2 * tokens * features * RING * HD,
        moved=5 * MIB,
    )


def on_device(normed, w_qkv, w_out, doc_start, grad_y):
    row_id, col_id = lax.axis_index("row"), lax.axis_index("col")
    z_id, core = row_id // CORES, row_id % CORES
    x_id, y_id = col_id // RING, col_id % RING
    z_arg, core_arg = z_id.reshape(1), core.reshape(1)
    place_arg = jnp.concatenate([jnp.stack([x_id, y_id, core]), doc_start])

    x_blocks, dy_blocks = near_gather(normed, to_x), near_gather(grad_y, to_y)
    blocks = tied(x_blocks + dy_blocks, [])
    x_parts = ring_gather(stack_blocks(core_arg, blocks[:RING]), to_y)
    dy_parts = ring_gather(stack_blocks(core_arg, blocks[RING:]), to_x)
    (w_turn,) = tied([w_qkv], [x_parts[1]])
    w_rel_t = turn_weights(z_arg, w_turn)
    flat_parts = tied(flat(x_parts) + flat(dy_parts), [w_rel_t])

    def parts_of(arrays):
        count = len(arrays) // 2
        return [[a[0], a[1], (a[2], a[3]), a[4]] for a in (arrays[:count], arrays[count:])]

    x_parts, dy_parts = parts_of(flat_parts)
    x_t, dy_all = arrange(z_arg, x_parts, dy_parts)
    both, kv_mine = project(z_arg, x_parts, dy_parts, w_qkv, w_out, [x_t])

    grad_query, attention, grad_kv, grad_kv_other = attend(
        place_arg, both, swap_cores(kv_mine), normed.shape[0]
    )
    grads = pack_grads(z_arg, grad_query, grad_kv, swap_cores(grad_kv_other), attention)
    g_mine = ring_gather(grads, to_z)
    g_other = [
        tuple(swap_cores(p) for p in part) if isinstance(part, tuple) else swap_cores(part)
        for part in g_mine
    ]

    grad_out = grad_out_product(z_arg, g_mine, g_other, dy_all)
    layer_out = scatter_sum_col(
        z_arg, core_arg, g_mine, g_other, w_out, piece_x, to_x, to_y, [grad_out]
    )
    grad_x = scatter_sum_col(z_arg, core_arg, g_mine, g_other, w_rel_t, piece_y, to_y, to_x)
    grad_qkv = grad_qkv_product(z_arg, x_t, g_mine, g_other)
    return (layer_out, grad_x, grad_qkv, grad_out)


def solution(mesh):
    in_specs = (P("col", "row"), P(None, "row", "col"), P("col", "row"), P(), P("col", "row"))
    out_specs = (P("col", "row"), P("col", "row"), P(None, "row", "col"), P("col", "row"))
    return jax.shard_map(
        on_device, mesh=mesh, in_specs=in_specs, out_specs=out_specs, check_vma=False
    )
```

```python
import math

import jax
import jax.numpy as jnp
from jax import lax
from jax.experimental import pallas as pl
from jax.experimental.pallas import tpu as pltpu
from jax.sharding import PartitionSpec as P

HD = 128
BLOCK = 128
NEG = -1e30
F32 = jnp.float32
BF16 = jnp.bfloat16
NT = (((1,), (1,)), ((), ()))
TN = (((0,), (0,)), ((), ()))
MIB = 1024 * 1024

RING = 4
CORES = 2
QKV = 3


def to_x(value, step):
    pairs = [(c, (c // RING + step) % RING * RING + c % RING) for c in range(RING * RING)]
    return lax.ppermute(value, "col", pairs)


def to_y(value, step):
    pairs = [(c, c // RING * RING + (c % RING + step) % RING) for c in range(RING * RING)]
    return lax.ppermute(value, "col", pairs)


def to_z(value, step):
    pairs = [(r, (r // CORES + step) % RING * CORES + r % CORES) for r in range(RING * CORES)]
    return lax.ppermute(value, "row", pairs)


def swap_cores(value):
    pairs = [(r, r // CORES * CORES + 1 - r % CORES) for r in range(RING * CORES)]
    return lax.ppermute(value, "row", pairs)


def tied(values, others):
    out = lax.optimization_barrier((tuple(values), tuple(others)))
    return list(out[0])


def mm(a, b):
    return jnp.dot(a, b, preferred_element_type=F32)


def whole(array):
    return pl.BlockSpec(array.shape, lambda i, s: (0,) * array.ndim)


def shape_of(array_shape, dtype):
    return jax.ShapeDtypeStruct(array_shape, dtype)


def call(
    kernel,
    scalar,
    inputs,
    in_specs,
    out_shape,
    out_specs,
    grid=1,
    flops=0,
    moved=0,
    scratch=(),
    limit=16,
    after=(),
):
    count = len(inputs)

    def wrapped(scalar_ref, *refs):
        kernel(scalar_ref, *refs[:count], *refs[count + len(after) :])

    inputs = list(inputs) + list(after)
    in_specs = list(in_specs) + [pl.BlockSpec(memory_space=pl.ANY)] * len(after)
    return pl.pallas_call(
        wrapped,
        grid_spec=pltpu.PrefetchScalarGridSpec(
            num_scalar_prefetch=1,
            grid=(grid,),
            in_specs=in_specs,
            out_specs=out_specs,
            scratch_shapes=list(scratch),
        ),
        out_shape=out_shape,
        compiler_params=pltpu.CompilerParams(vmem_limit_bytes=limit * MIB),
        cost_estimate=pl.CostEstimate(flops=flops, bytes_accessed=moved, transcendentals=0),
    )(scalar, *inputs)


def turn_weights(z_arg, w_qkv):
    count, depth, width = w_qkv.shape

    def kernel(z_ref, w_ref, out_ref):
        for which in range(count):
            out_ref[which * HD : (which + 1) * HD, :] = w_ref[which].T

    return call(
        kernel,
        z_arg,
        [w_qkv],
        [pl.BlockSpec((count, depth, HD), lambda d, z: (0, 0, (z[0] + d) % RING))],
        shape_of((count * width, depth), BF16),
        pl.BlockSpec((count * HD, depth), lambda d, z: (d, 0)),
        grid=RING,
        moved=4 * count * depth * width,
    )


def stack_blocks(core_arg, blocks):
    rows, width = blocks[0].shape
    half = rows // 2

    def kernel(core_ref, *refs):
        out_ref = refs[RING]
        for side in range(2):
            start = pl.multiple_of((core_ref[0] ^ side) * half, half)
            for i in range(RING):
                place = (side * RING + i) * half
                out_ref[place : place + half, :] = refs[i][pl.ds(start, half), :]

    out = shape_of((RING * rows, width), BF16)
    return call(
        kernel, core_arg, blocks, [whole(b) for b in blocks], out, whole(out), moved=8 * rows * width * 2
    )


def ring_gather(block, send):
    half = block.shape[0] // 2
    before, after = send(block, 1), send(block, -1)
    far = (send(before[:half], 1), send(after[half:], -1))
    return [block, after, far, before]


def near_gather(block, send):
    return [block] + [send(block, -step) for step in range(1, RING)]


def halves(parts, side, width=None, column=lambda i: 0):
    arrays, specs = [], []
    for part in parts:
        array, place = (part[side], 0) if isinstance(part, tuple) else (part, side)
        rows = array.shape[0] if isinstance(part, tuple) else array.shape[0] // 2
        arrays.append(array)
        specs.append(
            pl.BlockSpec(
                (rows, width or array.shape[1]), lambda i, s, place=place: (place, column(i))
            )
        )
    return arrays, specs


def flat(parts):
    return [array for part in parts for array in (part if isinstance(part, tuple) else (part,))]


def joined(parts, refs):
    values, refs = [], list(refs)
    for part in parts:
        if isinstance(part, tuple):
            values.append(jnp.concatenate([refs.pop(0)[...] for _ in part], axis=0))
        else:
            values.append(refs.pop(0)[...])
    return values


def by_place(refs, rows):
    return jnp.concatenate(
        [refs[dx][dy * rows : (dy + 1) * rows, :] for dy in range(RING) for dx in range(RING)], axis=0
    )


def head_products(z_arg, x_parts, dy_parts, w_qkv, w_out, side, dtype):
    count, depth, _ = w_qkv.shape
    x_arrays, x_specs = halves(x_parts, side)
    dy_arrays, dy_specs = halves(dy_parts, side)
    part = dy_specs[0].block_shape[0] // RING
    tokens = part * RING * RING
    width = (count + 1) * HD

    def kernel(z_ref, *refs):
        x_refs, dy_refs, (w_ref, wo_ref) = refs[:RING], refs[RING : 2 * RING], refs[2 * RING : 2 * RING + 2]
        out_refs = refs[2 * RING + 2 :]
        x = jnp.concatenate([ref[...] for ref in x_refs], axis=0)
        dy = by_place(dy_refs, part)
        places = [
            pl.ds(pl.multiple_of(lax.rem(z_ref[0] + step, RING) * HD, HD), HD) for step in range(RING)
        ]
        for pair in ((2, 1), (3, 0)):
            w = jnp.concatenate(
                [w_ref[which, :, places[step]] for step in pair for which in range(count)], axis=1
            )
            wo = jnp.concatenate([wo_ref[places[step], :] for step in pair], axis=0)
            prod = mm(x, w)
            prod_out = lax.dot_general(dy, wo, NT, preferred_element_type=F32)
            for i, step in enumerate(pair):
                out_refs[step][:, : count * HD] = prod[
                    :, i * count * HD : (i + 1) * count * HD
                ].astype(dtype)
                out_refs[step][:, count * HD :] = prod_out[:, i * HD : (i + 1) * HD].astype(dtype)

    outs = [shape_of((tokens, width), dtype) for _ in range(RING)]
    return call(
        kernel,
        z_arg,
        x_arrays + dy_arrays + [w_qkv, w_out],
        x_specs + dy_specs + [whole(w_qkv), whole(w_out)],
        outs,
        [whole(o) for o in outs],
        flops=2 * tokens * depth * width * RING,
        moved=8 * MIB,
        limit=24,
    )


def small(kernel, scalar, inputs, outs, after=()):
    moved = sum(a.size * a.dtype.itemsize for a in list(inputs) + list(outs))
    return call(
        kernel,
        scalar,
        inputs,
        [whole(a) for a in inputs],
        outs,
        [whole(o) for o in outs],
        moved=moved,
        after=after,
    )


def first_pieces(scalar, own, got):
    half, width = own.shape[0] // 2, own.shape[1]

    def kernel(s_ref, own_ref, got_ref, top_ref, low_ref):
        total = (own_ref[...] + got_ref[...].astype(F32)).astype(BF16)
        top_ref[...] = total[:half]
        low_ref[...] = total[half:]

    return small(kernel, scalar, [own, got], [shape_of((half, width), BF16)] * 2)


def second_pieces(scalar, one, got_one, top, three, got_three, low):
    half = top.shape[0]

    def kernel(s_ref, one_ref, got_one_ref, top_ref, three_ref, got_three_ref, low_ref, out1, out3):
        first = one_ref[...] + got_one_ref[...].astype(F32)
        out1[:half, :] = (first[:half] + top_ref[...].astype(F32)).astype(BF16)
        out1[half:, :] = first[half:].astype(BF16)
        second = three_ref[...] + got_three_ref[...].astype(F32)
        out3[:half, :] = second[:half].astype(BF16)
        out3[half:, :] = (second[half:] + low_ref[...].astype(F32)).astype(BF16)

    inputs = [one, got_one, top, three, got_three, low]
    return small(kernel, scalar, inputs, [shape_of(one.shape, BF16)] * 2)


def own_piece(scalar, own, got, one, three, after):
    def kernel(s_ref, own_ref, got_ref, one_ref, three_ref, out_ref, kv_ref):
        total = own_ref[...] + got_ref[...].astype(F32)
        total = total + one_ref[...].astype(F32) + three_ref[...].astype(F32)
        total = total.astype(BF16)
        out_ref[...] = total
        kv_ref[...] = total[:, HD : 3 * HD]

    outs = [shape_of(own.shape, BF16), shape_of((own.shape[0], 2 * HD), BF16)]
    return small(kernel, scalar, [own, got, one, three], outs, after)


def project(z_arg, x_parts, dy_parts, w_qkv, w_out, meanwhile):
    sent = head_products(z_arg, x_parts, dy_parts, w_qkv, w_out, 1, BF16)
    got = {step: swap_cores(sent[step]) for step in (2, 1, 3, 0)}
    own = head_products(z_arg, x_parts, dy_parts, w_qkv, w_out, 0, BF16)
    top, low = first_pieces(z_arg, own[2], got[2])
    top, low = to_z(top, 1), to_z(low, -1)
    one, three = second_pieces(z_arg, own[1], got[1], top, own[3], got[3], low)
    one, three = to_z(one, 1), to_z(three, -1)
    return own_piece(z_arg, own[0], got[0], one, three, meanwhile)


def arrange(scalar, x_parts, dy_parts):
    features = x_parts[0].shape[1]
    tokens = 4 * x_parts[0].shape[0]
    tile = 256
    arrays, specs = [], []
    for parts in (x_parts, dy_parts):
        for side in range(2):
            side_arrays, side_specs = halves(parts, side, tile, lambda i: i)
            arrays += side_arrays
            specs += side_specs
    part = specs[0].block_shape[0] // RING

    def kernel(s_ref, *refs):
        x_t_ref, dy_ref = refs[4 * RING :]
        x = jnp.concatenate([ref[...] for ref in refs[: 2 * RING]], axis=0)
        x_t_ref[...] = x.T
        for side in range(2):
            group = refs[(2 + side) * RING : (3 + side) * RING]
            dy_ref[side * tokens // 2 : (side + 1) * tokens // 2, :] = by_place(group, part)

    return call(
        kernel,
        scalar,
        arrays,
        specs,
        [shape_of((features, tokens), BF16), shape_of((tokens, features), BF16)],
        [
            pl.BlockSpec((tile, tokens), lambda i, s: (i, 0)),
            pl.BlockSpec((tokens, tile), lambda i, s: (0, i)),
        ],
        grid=features // tile,
        moved=8 * tokens * features,
    )


def attend(scalar, both, kv_other, tok_col):
    tokens = both.shape[0]
    scale = 1.0 / math.sqrt(HD)
    tile = 128
    part = tok_col // 2

    def kernel(s_ref, both_ref, other_ref, query_out, attn_out, own_out, other_out, probs_all, grads_all):
        def position(index, half):
            dy, dx, token = index // (RING * part), index // part % RING, index % part
            device = (s_ref[0] + dx) % RING * RING + (s_ref[1] + dy) % RING
            return device * tok_col + half * part + token

        side = s_ref[2]
        key_index = lax.broadcasted_iota(jnp.int32, (1, 2 * tokens), 1)
        key_pos = position(key_index % tokens, side ^ (key_index // tokens))
        keys = jnp.concatenate([both_ref[:, HD : 2 * HD], other_ref[:, :HD]], axis=0)
        values = jnp.concatenate([both_ref[:, 2 * HD : 3 * HD], other_ref[:, HD:]], axis=0)
        for start in range(0, tokens, tile):
            rows = slice(start, start + tile)
            queries, grad_rows = both_ref[rows, :HD], both_ref[rows, 3 * HD :]
            query_index = start + lax.broadcasted_iota(jnp.int32, (tile, 1), 0)
            query_pos = position(query_index, side)
            first_pos = jnp.zeros_like(query_pos)
            for block in range(s_ref.shape[0] - 3):
                first_pos = jnp.where(query_pos // BLOCK == block, s_ref[3 + block], first_pos)
            allowed = (key_pos >= first_pos) & (key_pos <= query_pos)
            scores = lax.dot_general(queries, keys, NT, preferred_element_type=F32) * scale
            scores = jnp.where(allowed, scores, NEG)
            row_max = jnp.max(scores, axis=1, keepdims=True)
            weights = jnp.where(allowed, jnp.exp(scores - row_max), 0.0)
            row_sum = jnp.sum(weights, axis=1, keepdims=True)
            attention = (mm(weights.astype(BF16), values) / row_sum).astype(BF16)
            attn_out[rows, :] = attention
            row_delta = jnp.sum(
                grad_rows.astype(F32) * attention.astype(F32), axis=1, keepdims=True
            )
            probs = weights * (1.0 / row_sum)
            grad_probs = lax.dot_general(grad_rows, values, NT, preferred_element_type=F32)
            grad_scores = (probs * (grad_probs - row_delta)).astype(BF16)
            query_out[rows, :] = (mm(grad_scores, keys) * scale).astype(BF16)
            probs_all[rows, :] = probs.astype(BF16)
            grads_all[rows, :] = grad_scores
        grad_keys = (
            lax.dot_general(grads_all[...], both_ref[:, :HD], TN, preferred_element_type=F32) * scale
        )
        grad_values = lax.dot_general(
            probs_all[...], both_ref[:, 3 * HD :], TN, preferred_element_type=F32
        )
        own_out[:, :HD] = grad_keys[:tokens]
        own_out[:, HD:] = grad_values[:tokens]
        other_out[:, :HD] = grad_keys[tokens:].astype(BF16)
        other_out[:, HD:] = grad_values[tokens:].astype(BF16)

    outs = [
        shape_of((tokens, HD), BF16),
        shape_of((tokens, HD), BF16),
        shape_of((tokens, 2 * HD), F32),
        shape_of((tokens, 2 * HD), BF16),
    ]
    return call(
        kernel,
        scalar,
        [both, kv_other],
        [whole(both), whole(kv_other)],
        outs,
        [whole(o) for o in outs],
        flops=14 * tokens * 2 * tokens * HD,
        moved=4 * MIB,
        scratch=[pltpu.VMEM((tokens, 2 * tokens), BF16), pltpu.VMEM((tokens, 2 * tokens), BF16)],
    )


def pack_grads(scalar, grad_query, own, got, attention):
    def kernel(s_ref, query_ref, own_ref, got_ref, attn_ref, out_ref):
        out_ref[:, :HD] = query_ref[...]
        out_ref[:, HD : 3 * HD] = (own_ref[...] + got_ref[...].astype(F32)).astype(BF16)
        out_ref[:, 3 * HD :] = attn_ref[...]

    inputs = [grad_query, own, got, attention]
    (out,) = small(kernel, scalar, inputs, [shape_of((grad_query.shape[0], 4 * HD), BF16)])
    return out


def piece_y(scalar, mine, other, weights, step, received, dtype, cut, after):
    rows = mine[0].shape[0] // RING
    width = QKV * HD
    depth, features = weights.shape
    arrays, specs = [], []
    for part in mine + other:
        if isinstance(part, tuple):
            count = part[0].shape[0] // rows
            array, place = part[step // count], step % count
        else:
            array, place = part, step
        arrays.append(array)
        specs.append(pl.BlockSpec((rows, width), lambda i, s, place=place: (place, 0)))

    def kernel(s_ref, *refs):
        top = jnp.concatenate([ref[...] for ref in refs[:RING]], axis=1)
        low = jnp.concatenate([ref[...] for ref in refs[RING : 2 * RING]], axis=1)
        prod = mm(jnp.concatenate([top, low], axis=0), refs[2 * RING][...])
        finish_piece(prod, refs[2 * RING + 1 :], step, received, dtype, cut)

    return piece_call(
        kernel,
        scalar,
        arrays + [weights],
        specs + [whole(weights)],
        (2 * rows, features),
        depth,
        received,
        dtype,
        cut,
        after,
    )


def finish_piece(prod, refs, step, received, dtype, cut):
    half = prod.shape[0] // 2
    top, low = prod[:half], prod[half:]
    if received:
        if step == 1:
            top = top + refs[0][...].astype(F32)
        else:
            low = low + refs[0][...].astype(F32)
    outs = refs[len(received) :]
    if cut:
        outs[0][...] = top.astype(dtype)
        outs[1][...] = low.astype(dtype)
    else:
        outs[0][:half, :] = top.astype(dtype)
        outs[0][half:, :] = low.astype(dtype)


def piece_call(kernel, scalar, inputs, specs, shape, depth, received, dtype, cut, after):
    rows, features = shape
    outs = [shape_of((rows // 2, features), dtype)] * 2 if cut else [shape_of(shape, dtype)]
    return call(
        kernel,
        scalar,
        inputs + received,
        specs + [whole(r) for r in received],
        outs,
        [whole(o) for o in outs],
        flops=2 * rows * depth * features,
        moved=2 * depth * (rows + features),
        after=after,
    )


def piece_x(z_arg, mine, other, w_out, step, received, dtype, cut, after):
    rows = mine[0].shape[0] // (RING * RING)
    depth, features = w_out.shape

    arrays = flat(mine) + flat(other)
    count = len(arrays) // 2

    def kernel(z_ref, *refs):
        def taken(parts, group):
            return jnp.concatenate(
                [
                    jnp.concatenate(
                        [
                            value[(dy * RING + step) * rows : (dy * RING + step + 1) * rows]
                            for dy in range(RING)
                        ],
                        axis=0,
                    )
                    for value in joined(parts, group)
                ],
                axis=1,
            )

        both = jnp.concatenate(
            [taken(mine, refs[:count]), taken(other, refs[count : 2 * count])], axis=0
        )
        w = jnp.concatenate([ref[...] for ref in refs[2 * count : 2 * count + RING]], axis=0)
        finish_piece(mm(both, w), refs[2 * count + RING :], step, received, dtype, cut)

    specs = [pl.BlockSpec((a.shape[0], HD), lambda i, z: (0, QKV)) for a in arrays]
    w_specs = [
        pl.BlockSpec((HD, features), lambda i, z, d=d: ((z[0] + d) % RING, 0)) for d in range(RING)
    ]
    return piece_call(
        kernel,
        z_arg,
        arrays + [w_out] * RING,
        specs + w_specs,
        (2 * rows * RING, features),
        depth,
        received,
        dtype,
        cut,
        after,
    )


def split_sum(scalar, own, arrived):
    rows, width = own.shape
    part = rows // (2 * RING)

    def kernel(s_ref, own_ref, *refs):
        outs = refs[len(arrived) :]
        for i, out_ref in enumerate(outs):
            for side in range(2):
                place = pl.ds((side * RING + i) * part, part)
                total = own_ref[place, :]
                for ref in refs[: len(arrived)]:
                    total = total + ref[place, :].astype(F32)
                out_ref[side * part : (side + 1) * part, :] = total.astype(out_ref.dtype)

    outs = [shape_of((2 * part, width), BF16 if i else F32) for i in range(RING)]
    inputs = [own] + arrived
    return call(
        kernel,
        scalar,
        inputs,
        [whole(a) for a in inputs],
        outs,
        [whole(o) for o in outs],
        moved=14 * rows * width,
    )


def last_sum(core_arg, own, arrived):
    rows, width = own.shape
    half = rows // 2

    def kernel(core_ref, own_ref, *refs):
        out_ref = refs[len(arrived)]
        total = own_ref[...]
        for ref in refs[: len(arrived)]:
            total = total + ref[...].astype(F32)
        for side in range(2):
            start = pl.multiple_of((core_ref[0] ^ side) * half, half)
            out_ref[pl.ds(start, half), :] = total[side * half : (side + 1) * half].astype(BF16)

    out = shape_of((rows, width), BF16)
    inputs = [own] + arrived
    return call(
        kernel, core_arg, inputs, [whole(a) for a in inputs], out, whole(out), moved=14 * rows * width
    )


def scatter_sum_col(z_arg, core_arg, mine, other, weights, piece, first, second, after=()):
    def product(step, received, dtype, cut=False, after=()):
        return piece(z_arg, mine, other, weights, step, received, dtype, cut, after)

    top, low = product(2, [], BF16, cut=True)
    top, low = first(top, 1), first(low, -1)
    (one,) = product(1, [top], BF16)
    one = first(one, 1)
    (three,) = product(3, [low], BF16)
    three = first(three, -1)
    (own,) = product(0, [], F32, after=after)
    own, *parts = split_sum(z_arg, own, [one, three])
    return last_sum(core_arg, own, [second(parts[step - 1], step) for step in (2, 1, 3)])


def grad_qkv_product(z_arg, x_t, g_mine, g_other):
    features, tokens = x_t.shape
    tile = 256
    width = QKV * HD
    g_arrays = flat(g_mine) + flat(g_other)

    def kernel(z_ref, x_ref, *refs):
        g_refs, out_ref = refs[:-1], refs[-1]
        mine = joined(g_mine, g_refs[: len(g_refs) // 2])
        other = joined(g_other, g_refs[len(g_refs) // 2 :])
        for first in range(0, RING, 2):
            g = jnp.concatenate(
                [
                    jnp.concatenate([group[first], group[first + 1]], axis=1)
                    for group in (mine, other)
                ],
                axis=0,
            )
            prod = mm(x_ref[...], g)
            for step in range(2):
                head = lax.rem(z_ref[0] + first + step, RING)
                place = pl.ds(pl.multiple_of(head * HD, HD), HD)
                for which in range(QKV):
                    start = step * width + which * HD
                    out_ref[which, :, place] = prod[:, start : start + HD]

    return call(
        kernel,
        z_arg,
        [x_t] + g_arrays,
        [pl.BlockSpec((tile, tokens), lambda i, z: (i, 0))]
        + [pl.BlockSpec((g.shape[0], width), lambda i, z: (0, 0)) for g in g_arrays],
        shape_of((QKV, features, RING * HD), F32),
        pl.BlockSpec((QKV, tile, RING * HD), lambda i, z: (0, i, 0)),
        grid=features // tile,
        flops=2 * tokens * features * RING * width,
        moved=12 * MIB,
    )


def grad_out_product(z_arg, g_mine, g_other, dy_all):
    tokens, features = dy_all.shape
    tile = 512
    g_arrays = flat(g_mine) + flat(g_other)

    def kernel(z_ref, *refs):
        g_refs, dy_ref, out_ref = refs[:-2], refs[-2], refs[-1]
        attn = jnp.concatenate(
            [
                jnp.concatenate(joined(parts, group), axis=1)
                for parts, group in (
                    (g_mine, g_refs[: len(g_refs) // 2]),
                    (g_other, g_refs[len(g_refs) // 2 :]),
                )
            ],
            axis=0,
        )
        prod = lax.dot_general(attn, dy_ref[...], TN, preferred_element_type=F32)
        for step in range(RING):
            head = lax.rem(z_ref[0] + step, RING)
            out_ref[pl.ds(pl.multiple_of(head * HD, HD), HD), :] = prod[step * HD : (step + 1) * HD]

    return call(
        kernel,
        z_arg,
        g_arrays + [dy_all],
        [pl.BlockSpec((g.shape[0], HD), lambda i, z: (0, QKV)) for g in g_arrays]
        + [pl.BlockSpec((tokens, tile), lambda i, z: (0, i))],
        shape_of((RING * HD, features), F32),
        pl.BlockSpec((RING * HD, tile), lambda i, z: (0, i)),
        grid=features // tile,
        flops=2 * tokens * features * RING * HD,
        moved=5 * MIB,
    )


def on_device(normed, w_qkv, w_out, doc_start, grad_y):
    row_id, col_id = lax.axis_index("row"), lax.axis_index("col")
    z_id, core = row_id // CORES, row_id % CORES
    x_id, y_id = col_id // RING, col_id % RING
    z_arg, core_arg = z_id.reshape(1), core.reshape(1)
    place_arg = jnp.concatenate([jnp.stack([x_id, y_id, core]), doc_start])

    x_blocks, dy_blocks = near_gather(normed, to_x), near_gather(grad_y, to_y)
    blocks = tied(x_blocks + dy_blocks, [])
    x_parts = ring_gather(stack_blocks(core_arg, blocks[:RING]), to_y)
    dy_parts = ring_gather(stack_blocks(core_arg, blocks[RING:]), to_x)
    (w_turn,) = tied([w_qkv], [x_parts[1]])
    w_rel_t = turn_weights(z_arg, w_turn)
    flat_parts = tied(flat(x_parts) + flat(dy_parts), [w_rel_t])

    def parts_of(arrays):
        count = len(arrays) // 2
        return [[a[0], a[1], (a[2], a[3]), a[4]] for a in (arrays[:count], arrays[count:])]

    x_parts, dy_parts = parts_of(flat_parts)
    x_t, dy_all = arrange(z_arg, x_parts, dy_parts)
    both, kv_mine = project(z_arg, x_parts, dy_parts, w_qkv, w_out, [x_t])

    grad_query, attention, grad_kv, grad_kv_other = attend(
        place_arg, both, swap_cores(kv_mine), normed.shape[0]
    )
    grads = pack_grads(z_arg, grad_query, grad_kv, swap_cores(grad_kv_other), attention)
    g_mine = ring_gather(grads, to_z)
    g_other = [
        tuple(swap_cores(p) for p in part) if isinstance(part, tuple) else swap_cores(part)
        for part in g_mine
    ]

    grad_out = grad_out_product(z_arg, g_mine, g_other, dy_all)
    layer_out = scatter_sum_col(
        z_arg, core_arg, g_mine, g_other, w_out, piece_x, to_x, to_y, [grad_out]
    )
    grad_x = scatter_sum_col(z_arg, core_arg, g_mine, g_other, w_rel_t, piece_y, to_y, to_x)
    grad_qkv = grad_qkv_product(z_arg, x_t, g_mine, g_other)
    return (layer_out, grad_x, grad_qkv, grad_out)


def solution(mesh):
    in_specs = (P("col", "row"), P(None, "row", "col"), P("col", "row"), P(), P("col", "row"))
    out_specs = (P("col", "row"), P("col", "row"), P(None, "row", "col"), P("col", "row"))
    return jax.shard_map(
        on_device, mesh=mesh, in_specs=in_specs, out_specs=out_specs, check_vma=False
    )
```

```python
import math

import jax
import jax.numpy as jnp
from jax import lax
from jax.experimental import pallas as pl
from jax.experimental.pallas import tpu as pltpu
from jax.sharding import PartitionSpec as P

HD = 128
BLOCK = 128
NEG = -1e30
F32 = jnp.float32
BF16 = jnp.bfloat16
NT = (((1,), (1,)), ((), ()))
TN = (((0,), (0,)), ((), ()))
MIB = 1024 * 1024

RING = 4
CORES = 2
QKV = 3


def to_x(value, step):
    pairs = [(c, (c // RING + step) % RING * RING + c % RING) for c in range(RING * RING)]
    return lax.ppermute(value, "col", pairs)


def to_y(value, step):
    pairs = [(c, c // RING * RING + (c % RING + step) % RING) for c in range(RING * RING)]
    return lax.ppermute(value, "col", pairs)


def to_z(value, step):
    pairs = [(r, (r // CORES + step) % RING * CORES + r % CORES) for r in range(RING * CORES)]
    return lax.ppermute(value, "row", pairs)


def swap_cores(value):
    pairs = [(r, r // CORES * CORES + 1 - r % CORES) for r in range(RING * CORES)]
    return lax.ppermute(value, "row", pairs)


def tied(values, others):
    out = lax.optimization_barrier((tuple(values), tuple(others)))
    return list(out[0])


def mm(a, b):
    return jnp.dot(a, b, preferred_element_type=F32)


def whole(array):
    return pl.BlockSpec(array.shape, lambda i, s: (0,) * array.ndim)


def shape_of(array_shape, dtype):
    return jax.ShapeDtypeStruct(array_shape, dtype)


def call(
    kernel,
    scalar,
    inputs,
    in_specs,
    out_shape,
    out_specs,
    grid=1,
    flops=0,
    moved=0,
    scratch=(),
    limit=16,
    after=(),
):
    count = len(inputs)

    def wrapped(scalar_ref, *refs):
        kernel(scalar_ref, *refs[:count], *refs[count + len(after) :])

    inputs = list(inputs) + list(after)
    in_specs = list(in_specs) + [pl.BlockSpec(memory_space=pl.ANY)] * len(after)
    return pl.pallas_call(
        wrapped,
        grid_spec=pltpu.PrefetchScalarGridSpec(
            num_scalar_prefetch=1,
            grid=(grid,),
            in_specs=in_specs,
            out_specs=out_specs,
            scratch_shapes=list(scratch),
        ),
        out_shape=out_shape,
        compiler_params=pltpu.CompilerParams(vmem_limit_bytes=limit * MIB),
        cost_estimate=pl.CostEstimate(flops=flops, bytes_accessed=moved, transcendentals=0),
    )(scalar, *inputs)


def turn_weights(z_arg, w_qkv):
    count, depth, width = w_qkv.shape

    def kernel(z_ref, w_ref, out_ref):
        for which in range(count):
            out_ref[which * HD : (which + 1) * HD, :] = w_ref[which].T

    return call(
        kernel,
        z_arg,
        [w_qkv],
        [pl.BlockSpec((count, depth, HD), lambda d, z: (0, 0, (z[0] + d) % RING))],
        shape_of((count * width, depth), BF16),
        pl.BlockSpec((count * HD, depth), lambda d, z: (d, 0)),
        grid=RING,
        moved=4 * count * depth * width,
    )


def stack_blocks(core_arg, blocks):
    rows, width = blocks[0].shape
    half = rows // 2

    def kernel(core_ref, *refs):
        out_ref = refs[RING]
        for side in range(2):
            start = pl.multiple_of((core_ref[0] ^ side) * half, half)
            for i in range(RING):
                place = (side * RING + i) * half
                out_ref[place : place + half, :] = refs[i][pl.ds(start, half), :]

    out = shape_of((RING * rows, width), BF16)
    return call(
        kernel, core_arg, blocks, [whole(b) for b in blocks], out, whole(out), moved=8 * rows * width * 2
    )


def ring_gather(block, send):
    half = block.shape[0] // 2
    before, after = send(block, 1), send(block, -1)
    far = (send(before[:half], 1), send(after[half:], -1))
    return [block, after, far, before]


def near_gather(block, send):
    return [block] + [send(block, -step) for step in range(1, RING)]


def halves(parts, side, width=None, column=lambda i: 0):
    arrays, specs = [], []
    for part in parts:
        array, place = (part[side], 0) if isinstance(part, tuple) else (part, side)
        rows = array.shape[0] if isinstance(part, tuple) else array.shape[0] // 2
        arrays.append(array)
        specs.append(
            pl.BlockSpec(
                (rows, width or array.shape[1]), lambda i, s, place=place: (place, column(i))
            )
        )
    return arrays, specs


def flat(parts):
    return [array for part in parts for array in (part if isinstance(part, tuple) else (part,))]


def joined(parts, refs):
    values, refs = [], list(refs)
    for part in parts:
        if isinstance(part, tuple):
            values.append(jnp.concatenate([refs.pop(0)[...] for _ in part], axis=0))
        else:
            values.append(refs.pop(0)[...])
    return values


def by_place(refs, rows):
    return jnp.concatenate(
        [refs[dx][dy * rows : (dy + 1) * rows, :] for dy in range(RING) for dx in range(RING)], axis=0
    )


def head_products(z_arg, x_parts, dy_parts, w_qkv, w_out, side, dtype):
    count, depth, _ = w_qkv.shape
    x_arrays, x_specs = halves(x_parts, side)
    dy_arrays, dy_specs = halves(dy_parts, side)
    part = dy_specs[0].block_shape[0] // RING
    tokens = part * RING * RING
    width = (count + 1) * HD

    def kernel(z_ref, *refs):
        x_refs, dy_refs, (w_ref, wo_ref) = refs[:RING], refs[RING : 2 * RING], refs[2 * RING : 2 * RING + 2]
        out_refs = refs[2 * RING + 2 :]
        x = jnp.concatenate([ref[...] for ref in x_refs], axis=0)
        dy = by_place(dy_refs, part)
        places = [
            pl.ds(pl.multiple_of(lax.rem(z_ref[0] + step, RING) * HD, HD), HD) for step in range(RING)
        ]
        for pair in ((2, 1), (3, 0)):
            w = jnp.concatenate(
                [w_ref[which, :, places[step]] for step in pair for which in range(count)], axis=1
            )
            wo = jnp.concatenate([wo_ref[places[step], :] for step in pair], axis=0)
            prod = mm(x, w)
            prod_out = lax.dot_general(dy, wo, NT, preferred_element_type=F32)
            for i, step in enumerate(pair):
                out_refs[step][:, : count * HD] = prod[
                    :, i * count * HD : (i + 1) * count * HD
                ].astype(dtype)
                out_refs[step][:, count * HD :] = prod_out[:, i * HD : (i + 1) * HD].astype(dtype)

    outs = [shape_of((tokens, width), dtype) for _ in range(RING)]
    return call(
        kernel,
        z_arg,
        x_arrays + dy_arrays + [w_qkv, w_out],
        x_specs + dy_specs + [whole(w_qkv), whole(w_out)],
        outs,
        [whole(o) for o in outs],
        flops=2 * tokens * depth * width * RING,
        moved=8 * MIB,
        limit=16,
    )


def small(kernel, scalar, inputs, outs, after=()):
    moved = sum(a.size * a.dtype.itemsize for a in list(inputs) + list(outs))
    return call(
        kernel,
        scalar,
        inputs,
        [whole(a) for a in inputs],
        outs,
        [whole(o) for o in outs],
        moved=moved,
        after=after,
    )


def first_pieces(scalar, own, got):
    half, width = own.shape[0] // 2, own.shape[1]

    def kernel(s_ref, own_ref, got_ref, top_ref, low_ref):
        total = (own_ref[...] + got_ref[...].astype(F32)).astype(BF16)
        top_ref[...] = total[:half]
        low_ref[...] = total[half:]

    return small(kernel, scalar, [own, got], [shape_of((half, width), BF16)] * 2)


def second_pieces(scalar, one, got_one, top, three, got_three, low):
    half = top.shape[0]

    def kernel(s_ref, one_ref, got_one_ref, top_ref, three_ref, got_three_ref, low_ref, out1, out3):
        first = one_ref[...] + got_one_ref[...].astype(F32)
        out1[:half, :] = (first[:half] + top_ref[...].astype(F32)).astype(BF16)
        out1[half:, :] = first[half:].astype(BF16)
        second = three_ref[...] + got_three_ref[...].astype(F32)
        out3[:half, :] = second[:half].astype(BF16)
        out3[half:, :] = (second[half:] + low_ref[...].astype(F32)).astype(BF16)

    inputs = [one, got_one, top, three, got_three, low]
    return small(kernel, scalar, inputs, [shape_of(one.shape, BF16)] * 2)


def own_piece(scalar, own, got, one, three, after):
    def kernel(s_ref, own_ref, got_ref, one_ref, three_ref, out_ref, kv_ref):
        total = own_ref[...] + got_ref[...].astype(F32)
        total = total + one_ref[...].astype(F32) + three_ref[...].astype(F32)
        total = total.astype(BF16)
        out_ref[...] = total
        kv_ref[...] = total[:, HD : 3 * HD]

    outs = [shape_of(own.shape, BF16), shape_of((own.shape[0], 2 * HD), BF16)]
    return small(kernel, scalar, [own, got, one, three], outs, after)


def project(z_arg, x_parts, dy_parts, w_qkv, w_out, meanwhile):
    sent = head_products(z_arg, x_parts, dy_parts, w_qkv, w_out, 1, BF16)
    got = {step: swap_cores(sent[step]) for step in (2, 1, 3, 0)}
    own = head_products(z_arg, x_parts, dy_parts, w_qkv, w_out, 0, F32)
    top, low = first_pieces(z_arg, own[2], got[2])
    top, low = to_z(top, 1), to_z(low, -1)
    one, three = second_pieces(z_arg, own[1], got[1], top, own[3], got[3], low)
    one, three = to_z(one, 1), to_z(three, -1)
    return own_piece(z_arg, own[0], got[0], one, three, meanwhile)


def arrange(scalar, x_parts, dy_parts):
    features = x_parts[0].shape[1]
    tokens = 4 * x_parts[0].shape[0]
    tile = 256
    arrays, specs = [], []
    for parts in (x_parts, dy_parts):
        for side in range(2):
            side_arrays, side_specs = halves(parts, side, tile, lambda i: i)
            arrays += side_arrays
            specs += side_specs
    part = specs[0].block_shape[0] // RING

    def kernel(s_ref, *refs):
        x_t_ref, dy_ref = refs[4 * RING :]
        x = jnp.concatenate([ref[...] for ref in refs[: 2 * RING]], axis=0)
        x_t_ref[...] = x.T
        for side in range(2):
            group = refs[(2 + side) * RING : (3 + side) * RING]
            dy_ref[side * tokens // 2 : (side + 1) * tokens // 2, :] = by_place(group, part)

    return call(
        kernel,
        scalar,
        arrays,
        specs,
        [shape_of((features, tokens), BF16), shape_of((tokens, features), BF16)],
        [
            pl.BlockSpec((tile, tokens), lambda i, s: (i, 0)),
            pl.BlockSpec((tokens, tile), lambda i, s: (0, i)),
        ],
        grid=features // tile,
        moved=8 * tokens * features,
    )


def attend(scalar, both, kv_other, tok_col):
    tokens = both.shape[0]
    scale = 1.0 / math.sqrt(HD)
    tile = 128
    part = tok_col // 2

    def kernel(s_ref, both_ref, other_ref, query_out, attn_out, own_out, other_out, probs_all, grads_all):
        def position(index, half):
            dy, dx, token = index // (RING * part), index // part % RING, index % part
            device = (s_ref[0] + dx) % RING * RING + (s_ref[1] + dy) % RING
            return device * tok_col + half * part + token

        side = s_ref[2]
        key_index = lax.broadcasted_iota(jnp.int32, (1, 2 * tokens), 1)
        key_pos = position(key_index % tokens, side ^ (key_index // tokens))
        keys = jnp.concatenate([both_ref[:, HD : 2 * HD], other_ref[:, :HD]], axis=0)
        values = jnp.concatenate([both_ref[:, 2 * HD : 3 * HD], other_ref[:, HD:]], axis=0)
        for start in range(0, tokens, tile):
            rows = slice(start, start + tile)
            queries, grad_rows = both_ref[rows, :HD], both_ref[rows, 3 * HD :]
            query_index = start + lax.broadcasted_iota(jnp.int32, (tile, 1), 0)
            query_pos = position(query_index, side)
            first_pos = jnp.zeros_like(query_pos)
            for block in range(s_ref.shape[0] - 3):
                first_pos = jnp.where(query_pos // BLOCK == block, s_ref[3 + block], first_pos)
            allowed = (key_pos >= first_pos) & (key_pos <= query_pos)
            scores = lax.dot_general(queries, keys, NT, preferred_element_type=F32) * scale
            scores = jnp.where(allowed, scores, NEG)
            row_max = jnp.max(scores, axis=1, keepdims=True)
            weights = jnp.where(allowed, jnp.exp(scores - row_max), 0.0)
            row_sum = jnp.sum(weights, axis=1, keepdims=True)
            attention = (mm(weights.astype(BF16), values) / row_sum).astype(BF16)
            attn_out[rows, :] = attention
            row_delta = jnp.sum(
                grad_rows.astype(F32) * attention.astype(F32), axis=1, keepdims=True
            )
            probs = weights * (1.0 / row_sum)
            grad_probs = lax.dot_general(grad_rows, values, NT, preferred_element_type=F32)
            grad_scores = (probs * (grad_probs - row_delta)).astype(BF16)
            query_out[rows, :] = (mm(grad_scores, keys) * scale).astype(BF16)
            probs_all[rows, :] = probs.astype(BF16)
            grads_all[rows, :] = grad_scores
        grad_keys = (
            lax.dot_general(grads_all[...], both_ref[:, :HD], TN, preferred_element_type=F32) * scale
        )
        grad_values = lax.dot_general(
            probs_all[...], both_ref[:, 3 * HD :], TN, preferred_element_type=F32
        )
        own_out[:, :HD] = grad_keys[:tokens]
        own_out[:, HD:] = grad_values[:tokens]
        other_out[:, :HD] = grad_keys[tokens:].astype(BF16)
        other_out[:, HD:] = grad_values[tokens:].astype(BF16)

    outs = [
        shape_of((tokens, HD), BF16),
        shape_of((tokens, HD), BF16),
        shape_of((tokens, 2 * HD), F32),
        shape_of((tokens, 2 * HD), BF16),
    ]
    return call(
        kernel,
        scalar,
        [both, kv_other],
        [whole(both), whole(kv_other)],
        outs,
        [whole(o) for o in outs],
        flops=14 * tokens * 2 * tokens * HD,
        moved=4 * MIB,
        scratch=[pltpu.VMEM((tokens, 2 * tokens), BF16), pltpu.VMEM((tokens, 2 * tokens), BF16)],
    )


def pack_grads(scalar, grad_query, own, got, attention):
    def kernel(s_ref, query_ref, own_ref, got_ref, attn_ref, out_ref):
        out_ref[:, :HD] = query_ref[...]
        out_ref[:, HD : 3 * HD] = (own_ref[...] + got_ref[...].astype(F32)).astype(BF16)
        out_ref[:, 3 * HD :] = attn_ref[...]

    inputs = [grad_query, own, got, attention]
    (out,) = small(kernel, scalar, inputs, [shape_of((grad_query.shape[0], 4 * HD), BF16)])
    return out


def piece_y(scalar, mine, other, weights, step, received, dtype, cut, after):
    rows = mine[0].shape[0] // RING
    width = QKV * HD
    depth, features = weights.shape
    arrays, specs = [], []
    for part in mine + other:
        if isinstance(part, tuple):
            count = part[0].shape[0] // rows
            array, place = part[step // count], step % count
        else:
            array, place = part, step
        arrays.append(array)
        specs.append(pl.BlockSpec((rows, width), lambda i, s, place=place: (place, 0)))

    def kernel(s_ref, *refs):
        top = jnp.concatenate([ref[...] for ref in refs[:RING]], axis=1)
        low = jnp.concatenate([ref[...] for ref in refs[RING : 2 * RING]], axis=1)
        prod = mm(jnp.concatenate([top, low], axis=0), refs[2 * RING][...])
        finish_piece(prod, refs[2 * RING + 1 :], step, received, dtype, cut)

    return piece_call(
        kernel,
        scalar,
        arrays + [weights],
        specs + [whole(weights)],
        (2 * rows, features),
        depth,
        received,
        dtype,
        cut,
        after,
    )


def finish_piece(prod, refs, step, received, dtype, cut):
    half = prod.shape[0] // 2
    top, low = prod[:half], prod[half:]
    if received:
        if step == 1:
            top = top + refs[0][...].astype(F32)
        else:
            low = low + refs[0][...].astype(F32)
    outs = refs[len(received) :]
    if cut:
        outs[0][...] = top.astype(dtype)
        outs[1][...] = low.astype(dtype)
    else:
        outs[0][:half, :] = top.astype(dtype)
        outs[0][half:, :] = low.astype(dtype)


def piece_call(kernel, scalar, inputs, specs, shape, depth, received, dtype, cut, after):
    rows, features = shape
    outs = [shape_of((rows // 2, features), dtype)] * 2 if cut else [shape_of(shape, dtype)]
    return call(
        kernel,
        scalar,
        inputs + received,
        specs + [whole(r) for r in received],
        outs,
        [whole(o) for o in outs],
        flops=2 * rows * depth * features,
        moved=2 * depth * (rows + features),
        after=after,
    )


def piece_x(z_arg, mine, other, w_out, step, received, dtype, cut, after):
    rows = mine[0].shape[0] // (RING * RING)
    depth, features = w_out.shape

    arrays = flat(mine) + flat(other)
    count = len(arrays) // 2

    def kernel(z_ref, *refs):
        def taken(parts, group):
            return jnp.concatenate(
                [
                    jnp.concatenate(
                        [
                            value[(dy * RING + step) * rows : (dy * RING + step + 1) * rows]
                            for dy in range(RING)
                        ],
                        axis=0,
                    )
                    for value in joined(parts, group)
                ],
                axis=1,
            )

        both = jnp.concatenate(
            [taken(mine, refs[:count]), taken(other, refs[count : 2 * count])], axis=0
        )
        w = jnp.concatenate([ref[...] for ref in refs[2 * count : 2 * count + RING]], axis=0)
        finish_piece(mm(both, w), refs[2 * count + RING :], step, received, dtype, cut)

    specs = [pl.BlockSpec((a.shape[0], HD), lambda i, z: (0, QKV)) for a in arrays]
    w_specs = [
        pl.BlockSpec((HD, features), lambda i, z, d=d: ((z[0] + d) % RING, 0)) for d in range(RING)
    ]
    return piece_call(
        kernel,
        z_arg,
        arrays + [w_out] * RING,
        specs + w_specs,
        (2 * rows * RING, features),
        depth,
        received,
        dtype,
        cut,
        after,
    )


def split_sum(scalar, own, arrived):
    rows, width = own.shape
    part = rows // (2 * RING)

    def kernel(s_ref, own_ref, *refs):
        outs = refs[len(arrived) :]
        for i, out_ref in enumerate(outs):
            for side in range(2):
                place = pl.ds((side * RING + i) * part, part)
                total = own_ref[place, :]
                for ref in refs[: len(arrived)]:
                    total = total + ref[place, :].astype(F32)
                out_ref[side * part : (side + 1) * part, :] = total.astype(out_ref.dtype)

    outs = [shape_of((2 * part, width), BF16 if i else F32) for i in range(RING)]
    inputs = [own] + arrived
    return call(
        kernel,
        scalar,
        inputs,
        [whole(a) for a in inputs],
        outs,
        [whole(o) for o in outs],
        moved=14 * rows * width,
    )


def last_sum(core_arg, own, arrived):
    rows, width = own.shape
    half = rows // 2

    def kernel(core_ref, own_ref, *refs):
        out_ref = refs[len(arrived)]
        total = own_ref[...]
        for ref in refs[: len(arrived)]:
            total = total + ref[...].astype(F32)
        for side in range(2):
            start = pl.multiple_of((core_ref[0] ^ side) * half, half)
            out_ref[pl.ds(start, half), :] = total[side * half : (side + 1) * half].astype(BF16)

    out = shape_of((rows, width), BF16)
    inputs = [own] + arrived
    return call(
        kernel, core_arg, inputs, [whole(a) for a in inputs], out, whole(out), moved=14 * rows * width
    )


def scatter_sum_col(z_arg, core_arg, mine, other, weights, piece, first, second, after=()):
    def product(step, received, dtype, cut=False, after=()):
        return piece(z_arg, mine, other, weights, step, received, dtype, cut, after)

    top, low = product(2, [], BF16, cut=True)
    top, low = first(top, 1), first(low, -1)
    (one,) = product(1, [top], BF16)
    one = first(one, 1)
    (three,) = product(3, [low], BF16)
    three = first(three, -1)
    (own,) = product(0, [], F32, after=after)
    own, *parts = split_sum(z_arg, own, [one, three])
    return last_sum(core_arg, own, [second(parts[step - 1], step) for step in (2, 1, 3)])


def grad_qkv_product(z_arg, x_t, g_mine, g_other):
    features, tokens = x_t.shape
    tile = 256
    width = QKV * HD
    g_arrays = flat(g_mine) + flat(g_other)

    def kernel(z_ref, x_ref, *refs):
        g_refs, out_ref = refs[:-1], refs[-1]
        mine = joined(g_mine, g_refs[: len(g_refs) // 2])
        other = joined(g_other, g_refs[len(g_refs) // 2 :])
        for first in range(0, RING, 2):
            g = jnp.concatenate(
                [
                    jnp.concatenate([group[first], group[first + 1]], axis=1)
                    for group in (mine, other)
                ],
                axis=0,
            )
            prod = mm(x_ref[...], g)
            for step in range(2):
                head = lax.rem(z_ref[0] + first + step, RING)
                place = pl.ds(pl.multiple_of(head * HD, HD), HD)
                for which in range(QKV):
                    start = step * width + which * HD
                    out_ref[which, :, place] = prod[:, start : start + HD]

    return call(
        kernel,
        z_arg,
        [x_t] + g_arrays,
        [pl.BlockSpec((tile, tokens), lambda i, z: (i, 0))]
        + [pl.BlockSpec((g.shape[0], width), lambda i, z: (0, 0)) for g in g_arrays],
        shape_of((QKV, features, RING * HD), F32),
        pl.BlockSpec((QKV, tile, RING * HD), lambda i, z: (0, i, 0)),
        grid=features // tile,
        flops=2 * tokens * features * RING * width,
        moved=12 * MIB,
    )


def grad_out_product(z_arg, g_mine, g_other, dy_all):
    tokens, features = dy_all.shape
    tile = 512
    g_arrays = flat(g_mine) + flat(g_other)

    def kernel(z_ref, *refs):
        g_refs, dy_ref, out_ref = refs[:-2], refs[-2], refs[-1]
        attn = jnp.concatenate(
            [
                jnp.concatenate(joined(parts, group), axis=1)
                for parts, group in (
                    (g_mine, g_refs[: len(g_refs) // 2]),
                    (g_other, g_refs[len(g_refs) // 2 :]),
                )
            ],
            axis=0,
        )
        prod = lax.dot_general(attn, dy_ref[...], TN, preferred_element_type=F32)
        for step in range(RING):
            head = lax.rem(z_ref[0] + step, RING)
            out_ref[pl.ds(pl.multiple_of(head * HD, HD), HD), :] = prod[step * HD : (step + 1) * HD]

    return call(
        kernel,
        z_arg,
        g_arrays + [dy_all],
        [pl.BlockSpec((g.shape[0], HD), lambda i, z: (0, QKV)) for g in g_arrays]
        + [pl.BlockSpec((tokens, tile), lambda i, z: (0, i))],
        shape_of((RING * HD, features), F32),
        pl.BlockSpec((RING * HD, tile), lambda i, z: (0, i)),
        grid=features // tile,
        flops=2 * tokens * features * RING * HD,
        moved=5 * MIB,
    )


def on_device(normed, w_qkv, w_out, doc_start, grad_y):
    row_id, col_id = lax.axis_index("row"), lax.axis_index("col")
    z_id, core = row_id // CORES, row_id % CORES
    x_id, y_id = col_id // RING, col_id % RING
    z_arg, core_arg = z_id.reshape(1), core.reshape(1)
    place_arg = jnp.concatenate([jnp.stack([x_id, y_id, core]), doc_start])

    x_blocks, dy_blocks = near_gather(normed, to_x), near_gather(grad_y, to_y)
    blocks = tied(x_blocks + dy_blocks, [])
    x_parts = ring_gather(stack_blocks(core_arg, blocks[:RING]), to_y)
    dy_parts = ring_gather(stack_blocks(core_arg, blocks[RING:]), to_x)
    (w_turn,) = tied([w_qkv], [x_parts[1]])
    w_rel_t = turn_weights(z_arg, w_turn)
    flat_parts = tied(flat(x_parts) + flat(dy_parts), [w_rel_t])

    def parts_of(arrays):
        count = len(arrays) // 2
        return [[a[0], a[1], (a[2], a[3]), a[4]] for a in (arrays[:count], arrays[count:])]

    x_parts, dy_parts = parts_of(flat_parts)
    x_t, dy_all = arrange(z_arg, x_parts, dy_parts)
    both, kv_mine = project(z_arg, x_parts, dy_parts, w_qkv, w_out, [x_t])

    grad_query, attention, grad_kv, grad_kv_other = attend(
        place_arg, both, swap_cores(kv_mine), normed.shape[0]
    )
    grads = pack_grads(z_arg, grad_query, grad_kv, swap_cores(grad_kv_other), attention)
    g_mine = ring_gather(grads, to_z)
    g_other = [
        tuple(swap_cores(p) for p in part) if isinstance(part, tuple) else swap_cores(part)
        for part in g_mine
    ]

    grad_out = grad_out_product(z_arg, g_mine, g_other, dy_all)
    layer_out = scatter_sum_col(
        z_arg, core_arg, g_mine, g_other, w_out, piece_x, to_x, to_y, [grad_out]
    )
    grad_x = scatter_sum_col(z_arg, core_arg, g_mine, g_other, w_rel_t, piece_y, to_y, to_x)
    grad_qkv = grad_qkv_product(z_arg, x_t, g_mine, g_other)
    return (layer_out, grad_x, grad_qkv, grad_out)


def solution(mesh):
    in_specs = (P("col", "row"), P(None, "row", "col"), P("col", "row"), P(), P("col", "row"))
    out_specs = (P("col", "row"), P("col", "row"), P(None, "row", "col"), P("col", "row"))
    return jax.shard_map(
        on_device, mesh=mesh, in_specs=in_specs, out_specs=out_specs, check_vma=False
    )
```
